512 devices in a mesh: grp: 8 (over x, core), seq: 16 (over z_hi, y), head: 4 (over z_lo).
Axes of the slice: x: 4, y: 4, z: 16 (z_hi: 4, z_lo: 4; z = z_hi * 4 + z_lo), core: 2. Of those that a mesh axis runs over, the one named last changes fastest.
Arguments:
- prompt_q: bfloat16 [14336, 8192], P(('grp', 'seq'), 'head'), parts along dimension 0, may hold values from -24 to 24
- prompt_k: bfloat16 [14336, 1024], P(('grp', 'seq'), 'head'), parts along dimension 0, may hold values from -24 to 24
- prompt_v: bfloat16 [14336, 1024], P(('grp', 'seq'), 'head'), parts along dimension 0, may hold values from -6 to 6
- resp_q: bfloat16 [128, 64, 8192], P(('grp', 'seq'), 'head'), parts along dimension 0, may hold values from -24 to 24
- resp_k: bfloat16 [128, 64, 1024], P(('grp', 'seq'), 'head'), parts along dimension 0, may hold values from -24 to 24
- resp_v: bfloat16 [128, 64, 1024], P(('grp', 'seq'), 'head'), parts along dimension 0, may hold values from -6 to 6
- lengths: int32 [128], P(('grp', 'seq')), parts along dimension 0, may hold values from 16 to 64, as said below
Outputs:
- prompt_out: bfloat16 [14336, 8192], P(('grp', 'seq'), 'head'), parts along dimension 0
- resp_out: bfloat16 [128, 64, 8192], P(('grp', 'seq'), 'head'), parts along dimension 0
The draws below stay inside these ranges and needn't reach their ends.
There are 8 independent parts, one for each index of `grp`. The reference program is written for one: setup_inputs(seed, part) draws one part's arguments, and reference() takes and returns one part's arrays. A program takes and returns all parts, laid end to end along the dimension named above; each array names one. Nothing has to cross between parts.
Inputs may be any that keep to these rules, and one draw needn't show every extreme that they name: `lengths`: in every draw one response has exactly 64 tokens and another exactly 16.
All inputs are finite; a program needn't handle non-finite values.
Results may differ from the reference program's by a relative error of at most 0.0075.
Values may be sent and summed in bfloat16 or wider, within the bound.
A program may use at most 64 MiB of HBM per device.

```python
import math
import jax
import jax.numpy as jnp
from jax import lax

Q_HEADS = 64
KV_HEADS = 8
HEAD_DIM = 128
LEN = 64
GROUP = 8
PROMPT = 1792
RESP = 16


def draw_prompt_q(key, part):
    key = jax.random.fold_in(key, 1)
    shape = (PROMPT, Q_HEADS * HEAD_DIM)
    values = jnp.clip(jax.random.normal(key, shape, jnp.float32), -6.0, 6.0)
    return values.astype(jnp.bfloat16)


def draw_prompt_k(key, part):
    key = jax.random.fold_in(key, 2)
    shape = (PROMPT, KV_HEADS * HEAD_DIM)
    values = 1.4 * jnp.clip(jax.random.normal(key, shape, jnp.float32), -6.0, 6.0)
    return values.astype(jnp.bfloat16)


def draw_resp_q(key, part):
    key = jax.random.fold_in(key, 3)
    row_count = RESP * LEN
    shape = (row_count, Q_HEADS * HEAD_DIM)
    values = jnp.clip(jax.random.normal(key, shape, jnp.float32), -6.0, 6.0)
    return values.reshape(RESP, LEN, Q_HEADS * HEAD_DIM).astype(jnp.bfloat16)


def draw_resp_k(key, part):
    key = jax.random.fold_in(key, 4)
    row_count = RESP * LEN
    shape = (row_count, KV_HEADS * HEAD_DIM)
    values = 1.4 * jnp.clip(jax.random.normal(key, shape, jnp.float32), -6.0, 6.0)
    return values.reshape(RESP, LEN, KV_HEADS * HEAD_DIM).astype(jnp.bfloat16)


def draw_lengths(key, part):
    key = jax.random.fold_in(key, 5)
    drawn = jax.random.randint(key, (RESP,), LEN // 4, LEN + 1)
    longest = jax.random.randint(jax.random.fold_in(key, 1), (), 0, RESP)
    step_over = jax.random.randint(jax.random.fold_in(key, 2), (), 1, RESP)
    shortest = (longest + step_over) % RESP
    drawn = drawn.at[longest].set(LEN)
    drawn = drawn.at[shortest].set(LEN // 4)
    return drawn.astype(jnp.int32)


def levels(key, shape, split, low, high):
    gain, own = 1.0, jax.random.fold_in(key, 6)
    for dim, shards_of in split:
        steps = jnp.exp(jax.random.uniform(jax.random.fold_in(own, dim), (shards_of,), jnp.float32, low / len(split), high / len(split)))
        gain = gain * jnp.repeat(steps, shape[dim] // shards_of).reshape([-1 if axis == dim else 1 for axis in range(len(shape))])
    return gain


def bell_draw(rng, dims, scale, most, shards=(), kind=jnp.bfloat16):
    values = scale * jax.random.normal(rng, dims, jnp.float32)
    if shards:
        values = values * levels(rng, dims, shards, -0.22, 0.18)
    return jnp.clip(values, -most, most).astype(kind)


def setup_inputs(seed: int = 0, part: int = 0) -> dict:
    streams_of = jax.random.split(jax.random.key(seed), 8)
    own_keys = jax.random.split(jax.random.fold_in(streams_of[7], part), 8)
    return {
        "prompt_q": draw_prompt_q(jax.random.fold_in(jax.random.fold_in(streams_of[7], part), 71), part),
        "prompt_k": draw_prompt_k(jax.random.fold_in(jax.random.fold_in(streams_of[7], part), 71), part),
        "prompt_v": bell_draw(own_keys[2], (PROMPT, KV_HEADS * HEAD_DIM), 1.0, 6.0, ((0, 16), (1, 4))),
        "resp_q": draw_resp_q(jax.random.fold_in(jax.random.fold_in(streams_of[7], part), 71), part),
        "resp_k": draw_resp_k(jax.random.fold_in(jax.random.fold_in(streams_of[7], part), 71), part),
        "resp_v": bell_draw(own_keys[5], (RESP, LEN, KV_HEADS * HEAD_DIM), 1.0, 6.0, ((0, 16), (1, 4))),
        "lengths": draw_lengths(jax.random.fold_in(jax.random.fold_in(streams_of[7], part), 71), part),
    }


very_low = -1e+30

def softmax_mix(queries, keys_in, values_in, visible):
    scores = jnp.einsum('gqd,nd->gqn', queries, keys_in) / math.sqrt(HEAD_DIM)
    masked = jnp.where(visible, scores, very_low)
    highest = lax.optimization_barrier(jnp.max(masked, axis=-1, keepdims=True))
    weights = jnp.where(visible, jnp.exp(masked - highest), 0.0)
    summed = lax.optimization_barrier(jnp.sum(weights, axis=-1, keepdims=True))
    rounded = lax.optimization_barrier(weights.astype(jnp.bfloat16)).astype(jnp.float32)
    mixed = jnp.einsum('gqn,nd->gqd', rounded, values_in)
    return mixed / summed

def reference(prompt_q, prompt_k, prompt_v, resp_q, resp_k, resp_v, lengths):
    queries = prompt_q.astype(jnp.float32).reshape(PROMPT, KV_HEADS, GROUP, HEAD_DIM).transpose(1, 2, 0, 3)
    keys_all = prompt_k.astype(jnp.float32).reshape(PROMPT, KV_HEADS, HEAD_DIM).transpose(1, 0, 2)
    values_all = prompt_v.astype(jnp.float32).reshape(PROMPT, KV_HEADS, HEAD_DIM).transpose(1, 0, 2)
    positions = jnp.arange(PROMPT)
    visible = positions[None, :] <= positions[:, None]
    mixed = lax.map(lambda member: softmax_mix(member[0], member[1], member[2], visible), (queries, keys_all, values_all))
    prompt_out = mixed.transpose(2, 0, 1, 3).reshape(PROMPT, Q_HEADS * HEAD_DIM).astype(jnp.bfloat16)
    steps_own = jnp.arange(LEN)
    causal = steps_own[None, :] <= steps_own[:, None]
    seen = jnp.concatenate([jnp.ones((LEN, PROMPT), bool), causal], axis=1)

    def one_response(member):
        own_q, own_k, own_v, length = member
        heads_q = own_q.astype(jnp.float32).reshape(LEN, KV_HEADS, GROUP, HEAD_DIM).transpose(1, 2, 0, 3)
        joined_k = jnp.concatenate([prompt_k, own_k], axis=0).astype(jnp.float32)
        joined_v = jnp.concatenate([prompt_v, own_v], axis=0).astype(jnp.float32)
        heads_k = joined_k.reshape(PROMPT + LEN, KV_HEADS, HEAD_DIM).transpose(1, 0, 2)
        heads_v = joined_v.reshape(PROMPT + LEN, KV_HEADS, HEAD_DIM).transpose(1, 0, 2)
        result = lax.map(lambda inner: softmax_mix(inner[0], inner[1], inner[2], seen), (heads_q, heads_k, heads_v))
        result = result.transpose(2, 0, 1, 3).reshape(LEN, Q_HEADS * HEAD_DIM)
        result = jnp.where((steps_own < length)[:, None], result, 0.0)
        return result.astype(jnp.bfloat16)
    resp_out = lax.map(one_response, (resp_q, resp_k, resp_v, lengths))
    return (prompt_out, resp_out)
```

```python
import functools
import math

import jax
import jax.numpy as jnp
from jax import lax
from jax.experimental import pallas as pl
from jax.experimental.pallas import tpu as pltpu
from jax.sharding import PartitionSpec as P

HEAD_DIM = 128
GROUP = 8
MESH = pl.DeviceIdType.MESH
SCALE = math.log2(math.e) / math.sqrt(HEAD_DIM)
very_low = -1e30

RING = 4


def kernel(
    sizes,
    pq_ref, pk_ref, pv_ref, rq_ref, rk_ref, rv_ref,
    po_ref, ro_ref,
    kbuf, vbuf, pq, rqb, rkb, rvb, qs, top, acc, pob, rob,
    send_sem, recv_sem, local_sem,
):
    rows, toks, parts = sizes
    kv = 2
    wide = GROUP * HEAD_DIM
    qwidth = kv * wide
    resp_rows = GROUP * parts * toks
    chunk = RING * rows

    seq = lax.axis_index("seq")
    head = lax.axis_index("head")
    zh, y = seq // RING, lax.rem(seq, RING)

    def at(dz, dy):
        return lax.rem(zh + dz + RING, RING) * RING + lax.rem(y + dy + RING, RING)

    z_next, z_prev = at(1, 0), at(-1, 0)
    y_next, y_prev = at(0, 1), at(0, -1)
    others = [lax.rem(head + d, parts) for d in range(1, parts)]

    barrier = pltpu.get_barrier_semaphore()
    for peer in (z_next, z_prev, y_next, y_prev):
        pl.semaphore_signal(barrier, inc=1, device_id={"seq": peer}, device_id_type=MESH)
    for peer in others:
        pl.semaphore_signal(barrier, inc=1, device_id={"head": peer}, device_id_type=MESH)

    def rows_of(dy):
        return pl.ds(pl.multiple_of(lax.rem(y + dy + RING, RING) * rows, 16), rows)

    def cols(x):
        return pl.ds(x * HEAD_DIM, HEAD_DIM)

    mine = rows_of(0)
    bufs, given = {"k": kbuf, "v": vbuf}, {"k": pk_ref, "v": pv_ref}

    local = []

    def bring(src, dst):
        copy = pltpu.make_async_copy(src, dst, local_sem.at[len(local)])
        copy.start()
        local.append(copy)
        return copy

    got_pq = bring(pq_ref, pq)
    got_kv = [bring(given[a], bufs[a].at[0, mine, :]) for a in "kv"]
    own_q = pl.ds(pl.multiple_of(head * qwidth, qwidth), qwidth)
    own_kv = pl.ds(pl.multiple_of(head * kv * HEAD_DIM, kv * HEAD_DIM), kv * HEAD_DIM)
    got_resp = [
        bring(rq_ref.at[:, own_q], rqb.at[head]),
        bring(rk_ref.at[:, own_kv], rkb.at[head]),
        bring(rv_ref.at[:, own_kv], rvb.at[head]),
    ]
    pl.semaphore_wait(barrier, 4 + len(others))

    sent = {}

    def send(name, src, dst, peer):
        copy = pltpu.make_async_remote_copy(
            src_ref=src,
            dst_ref=dst,
            send_sem=send_sem.at[len(sent)],
            recv_sem=recv_sem.at[len(sent)],
            device_id=peer,
            device_id_type=MESH,
        )
        copy.start()
        sent[name] = copy

    def arrived(name):
        sent[name].wait_recv()

    def z1(a, x, way):
        slot = 1 if way > 0 else 2
        send(
            ("z1", a, x, way), given[a].at[:, cols(x)], bufs[a].at[slot, mine, cols(x)],
            {"seq": z_next if way > 0 else z_prev},
        )

    def z2(a, x):
        slot, peer = (1, z_next) if a == "k" else (2, z_prev)
        send(
            ("z2", a, x), bufs[a].at[slot, mine, cols(x)], bufs[a].at[3, mine, cols(x)],
            {"seq": peer},
        )

    def y1(a, x, slot):
        place = bufs[a].at[slot, mine, cols(x)]
        src = given[a].at[:, cols(x)] if slot == 0 else place
        for way in (1, -1) if a == "k" else (-1, 1):
            send(("y1", a, x, slot, way), src, place, {"seq": y_next if way > 0 else y_prev})

    def y2(x, slot):
        for a, way in (("k", 1), ("v", -1)):
            arrived(("y1", a, x, slot, way))
            place = bufs[a].at[slot, rows_of(-way), cols(x)]
            send(("y2", a, x, slot), place, place, {"seq": y_next if way > 0 else y_prev})

    def whole(x, slot):
        for a, way in (("k", -1), ("v", 1)):
            arrived(("y1", a, x, slot, way))
        for a in "kv":
            arrived(("y2", a, x, slot))

    def swap_q(x):
        for d, peer in enumerate(others):
            begin = pl.multiple_of(peer * qwidth + x * wide, wide)
            send(
                ("q", x, d), rq_ref.at[:, pl.ds(begin, wide)],
                rqb.at[head, :, pl.ds(x * wide, wide)], {"head": peer},
            )

    def swap_kv():
        for d, peer in enumerate(others):
            begin = pl.multiple_of(peer * kv * HEAD_DIM, kv * HEAD_DIM)
            for name, src, dst in (("rk", rk_ref, rkb), ("rv", rv_ref, rvb)):
                send(
                    (name, d), src.at[:, pl.ds(begin, kv * HEAD_DIM)], dst.at[head],
                    {"head": peer},
                )

    def swap_out(x):
        to = pl.multiple_of(head * qwidth + x * wide, wide)
        for d, peer in enumerate(others):
            send(
                ("o", x, d), rob.at[peer, :, pl.ds(x * wide, wide)],
                ro_ref.at[:, pl.ds(to, wide)], {"head": peer},
            )
        bring(rob.at[head, :, pl.ds(x * wide, wide)], ro_ref.at[:, pl.ds(to, wide)])

    def attend(x, keys, values, begin, tile, count, first, visible):
        def body(i, carry):
            here = pl.ds(pl.multiple_of(begin + i * tile, 16), tile)
            k, v = keys(), values()
            scores = lax.dot_general(
                qs[x, here, :], k, (((1,), (1,)), ((), ())), preferred_element_type=jnp.float32
            )
            if visible is not None:
                scores = jnp.where(visible(scores.shape), scores, very_low)
            high = jnp.max(scores, axis=1, keepdims=True)
            if first:
                high = jnp.broadcast_to(high, (tile, HEAD_DIM))
            else:
                before = top[x, here, :]
                high = jnp.maximum(before, high)
            top[x, here, :] = high
            count_keys = k.shape[0]
            spread = jnp.concatenate([high] * -(-count_keys // HEAD_DIM), axis=1)[:, :count_keys]
            weights = jnp.exp2((scores - spread) * SCALE).astype(jnp.bfloat16)
            both = jnp.concatenate([v, jnp.ones_like(v)], axis=1)
            mixed = jnp.dot(weights, both, preferred_element_type=jnp.float32)
            if not first:
                factor = jnp.exp2((before - high) * SCALE)
                mixed = acc[x, here, :] * jnp.concatenate([factor, factor], axis=1) + mixed
            acc[x, here, :] = mixed
            return carry

        lax.fori_loop(0, count, body, 0)

    def block(buf, slot, x):
        return lambda: buf[slot, :, x * HEAD_DIM : (x + 1) * HEAD_DIM]

    per = parts * toks
    resp_tile, prompt_tile = 2 * per, rows

    def resp_slot(x, slot):
        attend(
            x, block(kbuf, slot, x), block(vbuf, slot, x), 0, resp_tile, resp_rows // resp_tile,
            False, None,
        )

    def resp_own(x):
        def flat(buf):
            return lambda: buf[:, :, x * HEAD_DIM : (x + 1) * HEAD_DIM].reshape(per, HEAD_DIM)

        def visible(shape):
            row = lax.rem(lax.broadcasted_iota(jnp.int32, shape, 0), per)
            return lax.broadcasted_iota(jnp.int32, shape, 1) <= row

        attend(x, flat(rkb), flat(rvb), 0, resp_tile, resp_rows // resp_tile, True, visible)

    def prompt_slot(x, slot):
        def visible(shape):
            row = lax.broadcasted_iota(jnp.int32, shape, 0) + y * rows
            return lax.broadcasted_iota(jnp.int32, shape, 1) <= row

        def run():
            attend(
                x, block(kbuf, slot, x), block(vbuf, slot, x), resp_rows, prompt_tile, GROUP,
                slot == 0, visible if slot == 0 else None,
            )

        if slot == 0:
            run()
        else:
            pl.when({1: zh >= 1, 2: zh == RING - 1, 3: zh >= 2}[slot])(run)

    def stack_prompt():
        for x in range(kv):
            for g in range(GROUP):
                at_col = (x * GROUP + g) * HEAD_DIM
                qs[x, pl.ds(resp_rows + g * rows, rows), :] = pq[:, at_col : at_col + HEAD_DIM]

    def stack_resp(x):
        for g in range(GROUP):
            at_col = (x * GROUP + g) * HEAD_DIM
            qs[x, pl.ds(g * per, per), :] = rqb[:, :, at_col : at_col + HEAD_DIM].reshape(
                per, HEAD_DIM
            )

    def quotient(x, begin, count):
        part = acc[x, pl.ds(begin, count), :]
        return (part[:, :HEAD_DIM] / part[:, HEAD_DIM:]).astype(jnp.bfloat16)

    def finish_resp(x):
        for g in range(GROUP):
            at_col = (x * GROUP + g) * HEAD_DIM
            rob[:, :, at_col : at_col + HEAD_DIM] = quotient(x, g * per, per).reshape(
                parts, toks, HEAD_DIM
            )

    def finish_prompt(x):
        for g in range(GROUP):
            at_col = (x * GROUP + g) * HEAD_DIM
            pob[:, at_col : at_col + HEAD_DIM] = quotient(x, resp_rows + g * rows, rows)
        part = pl.ds(x * wide, wide)
        bring(pob.at[:, part], po_ref.at[:, part])

    def first_sends(x):
        z1("k", x, 1)
        z1("v", x, -1)
        z1("v", x, 1)
        z1("k", x, -1)
        y1("k", x, 0)
        y1("v", x, 0)

    def after_z1(x):
        arrived(("z1", "k", x, 1))
        z2("k", x)
        y1("k", x, 1)
        arrived(("z1", "v", x, -1))
        z2("v", x)
        y1("v", x, 2)
        arrived(("z1", "v", x, 1))
        y1("v", x, 1)
        arrived(("z1", "k", x, -1))
        y1("k", x, 2)

    def after_z2(x):
        for a in "kv":
            arrived(("z2", a, x))
            y1(a, x, 3)

    def take_resp(x):
        if x == 0:
            for d in range(parts - 1):
                arrived(("rk", d))
                arrived(("rv", d))
        for d in range(parts - 1):
            arrived(("q", x, d))
        stack_resp(x)

    first_sends(0)
    swap_q(0)
    swap_kv()
    first_sends(1)
    swap_q(1)

    got_pq.wait()
    stack_prompt()
    for copy in got_kv + got_resp:
        copy.wait()
    y2(0, 0)
    y2(1, 0)
    whole(0, 0)
    prompt_slot(0, 0)
    after_z1(0)
    whole(1, 0)
    prompt_slot(1, 0)
    after_z1(1)
    y2(0, 1)
    y2(0, 2)
    take_resp(0)
    resp_own(0)
    resp_slot(0, 0)
    after_z2(0)
    y2(1, 1)
    y2(1, 2)
    whole(0, 1)
    resp_slot(0, 1)
    prompt_slot(0, 1)
    after_z2(1)
    y2(0, 3)
    whole(0, 2)
    resp_slot(0, 2)
    prompt_slot(0, 2)
    y2(1, 3)
    whole(0, 3)
    resp_slot(0, 3)
    finish_resp(0)
    swap_out(0)
    take_resp(1)
    resp_own(1)
    resp_slot(1, 0)
    whole(1, 1)
    resp_slot(1, 1)
    whole(1, 2)
    resp_slot(1, 2)
    whole(1, 3)
    resp_slot(1, 3)
    finish_resp(1)
    swap_out(1)
    prompt_slot(0, 3)
    finish_prompt(0)
    prompt_slot(1, 1)
    prompt_slot(1, 2)
    prompt_slot(1, 3)
    finish_prompt(1)
    for x in range(kv):
        for d in range(parts - 1):
            arrived(("o", x, d))
    for copy in sent.values():
        copy.wait_send()
    for copy in local[6:]:
        copy.wait()


def on_device(prompt_q, prompt_k, prompt_v, resp_q, resp_k, resp_v, lengths):
    rows, qwidth = prompt_q.shape
    kwidth = prompt_k.shape[1]
    toks = resp_q.shape[1]
    parts = lax.axis_size("head")
    kv = kwidth // HEAD_DIM
    total = GROUP * (rows + parts * toks)
    any_place = pl.BlockSpec(memory_space=pl.ANY)
    bf16 = jnp.bfloat16
    messages = 80
    prompt_out, mixed = pl.pallas_call(
        functools.partial(kernel, (rows, toks, parts)),
        out_shape=(
            jax.ShapeDtypeStruct((rows, qwidth), bf16),
            jax.ShapeDtypeStruct((toks, parts * qwidth), bf16),
        ),
        in_specs=[any_place] * 6,
        out_specs=(any_place, any_place),
        scratch_shapes=[
            pltpu.VMEM((RING, RING * rows, kwidth), bf16),
            pltpu.VMEM((RING, RING * rows, kwidth), bf16),
            pltpu.VMEM((rows, qwidth), bf16),
            pltpu.VMEM((parts, toks, qwidth), bf16),
            pltpu.VMEM((parts, toks, kwidth), bf16),
            pltpu.VMEM((parts, toks, kwidth), bf16),
            pltpu.VMEM((kv, total, HEAD_DIM), bf16),
            pltpu.VMEM((kv, total, HEAD_DIM), jnp.float32),
            pltpu.VMEM((kv, total, 2 * HEAD_DIM), jnp.float32),
            pltpu.VMEM((rows, qwidth), bf16),
            pltpu.VMEM((parts, toks, qwidth), bf16),
            pltpu.SemaphoreType.DMA((messages,)),
            pltpu.SemaphoreType.DMA((messages,)),
            pltpu.SemaphoreType.DMA((16,)),
        ],
        compiler_params=pltpu.CompilerParams(
            collective_id=0, has_side_effects=True, vmem_limit_bytes=48 * 1024 * 1024
        ),
    )(prompt_q, prompt_k, prompt_v, resp_q[0], resp_k[0], resp_v[0])
    positions = lax.axis_index("head") * toks + jnp.arange(toks)
    live = positions < lengths[0]
    resp_out = jnp.where(live[:, None], mixed, jnp.zeros_like(mixed))[None]
    return (prompt_out, resp_out)


def solution(mesh):
    placed = (
        P(("grp", "seq"), "head"),
        P(("grp", "seq"), "head"),
        P(("grp", "seq"), "head"),
        P(("grp", "seq"), "head", None),
        P(("grp", "seq"), "head", None),
        P(("grp", "seq"), "head", None),
        P(("grp", "seq")),
    )
    return jax.shard_map(
        on_device,
        mesh=mesh,
        in_specs=placed,
        out_specs=(P(("grp", "seq"), "head"), P(("grp", "seq"), "head", None)),
        check_vma=False,
    )
```

```python
import functools
import math

import jax
import jax.numpy as jnp
from jax import lax
from jax.experimental import pallas as pl
from jax.experimental.pallas import tpu as pltpu
from jax.sharding import PartitionSpec as P

HEAD_DIM = 128
GROUP = 8
MESH = pl.DeviceIdType.MESH
SCALE = math.log2(math.e) / math.sqrt(HEAD_DIM)
very_low = -1e30

RING = 4


def kernel(
    sizes,
    pq_ref, pk_ref, pv_ref, rq_ref, rk_ref, rv_ref,
    po_ref, ro_ref,
    kbuf, vbuf, pq, rqb, rkb, rvb, qs, top, acc, pob, rob,
    send_sem, recv_sem, local_sem,
):
    rows, toks, parts = sizes
    kv = 2
    wide = GROUP * HEAD_DIM
    qwidth = kv * wide
    resp_rows = GROUP * parts * toks
    chunk = RING * rows

    seq = lax.axis_index("seq")
    head = lax.axis_index("head")
    zh, y = seq // RING, lax.rem(seq, RING)

    def at(dz, dy):
        return lax.rem(zh + dz + RING, RING) * RING + lax.rem(y + dy + RING, RING)

    z_next, z_prev = at(1, 0), at(-1, 0)
    y_next, y_prev = at(0, 1), at(0, -1)
    others = [lax.rem(head + d, parts) for d in range(1, parts)]

    barrier = pltpu.get_barrier_semaphore()
    for peer in (z_next, z_prev, y_next, y_prev):
        pl.semaphore_signal(barrier, inc=1, device_id={"seq": peer}, device_id_type=MESH)
    for peer in others:
        pl.semaphore_signal(barrier, inc=1, device_id={"head": peer}, device_id_type=MESH)

    def rows_of(dy):
        return pl.ds(pl.multiple_of(lax.rem(y + dy + RING, RING) * rows, 16), rows)

    mine = rows_of(0)
    bufs, given = {"k": kbuf, "v": vbuf}, {"k": pk_ref, "v": pv_ref}

    local = []

    def bring(src, dst):
        copy = pltpu.make_async_copy(src, dst, local_sem.at[len(local)])
        copy.start()
        local.append(copy)
        return copy

    got_pq = bring(pq_ref, pq)
    got_kv = [
        bring(given[a].at[:, pl.ds(x * HEAD_DIM, HEAD_DIM)], bufs[a].at[0, x, mine])
        for x in range(kv)
        for a in "kv"
    ]
    own_q = pl.ds(pl.multiple_of(head * qwidth, qwidth), qwidth)
    own_kv = pl.ds(pl.multiple_of(head * kv * HEAD_DIM, kv * HEAD_DIM), kv * HEAD_DIM)
    got_resp = [
        bring(rq_ref.at[:, own_q], rqb.at[head]),
        bring(rk_ref.at[:, own_kv], rkb.at[head]),
        bring(rv_ref.at[:, own_kv], rvb.at[head]),
    ]
    pl.semaphore_wait(barrier, 4 + len(others))

    sent = {}

    def send(name, src, dst, peer):
        copy = pltpu.make_async_remote_copy(
            src_ref=src,
            dst_ref=dst,
            send_sem=send_sem.at[len(sent)],
            recv_sem=recv_sem.at[len(sent)],
            device_id=peer,
            device_id_type=MESH,
        )
        copy.start()
        sent[name] = copy

    def arrived(name):
        sent[name].wait_recv()

    def z1(a, x, way):
        slot = 1 if way > 0 else 2
        send(
            ("z1", a, x, way), bufs[a].at[0, x, mine], bufs[a].at[slot, x, mine],
            {"seq": z_next if way > 0 else z_prev},
        )

    def z2(a, x):
        slot, peer = (1, z_next) if a == "k" else (2, z_prev)
        send(
            ("z2", a, x), bufs[a].at[slot, x, mine], bufs[a].at[3, x, mine],
            {"seq": peer},
        )

    def y1(a, x, slot):
        place = bufs[a].at[slot, x, mine]
        for way in (1, -1) if a == "k" else (-1, 1):
            send(("y1", a, x, slot, way), place, place, {"seq": y_next if way > 0 else y_prev})

    def y2(x, slot):
        for a, way in (("k", 1), ("v", -1)):
            arrived(("y1", a, x, slot, way))
            place = bufs[a].at[slot, x, rows_of(-way)]
            send(("y2", a, x, slot), place, place, {"seq": y_next if way > 0 else y_prev})

    def whole(x, slot):
        for a, way in (("k", -1), ("v", 1)):
            arrived(("y1", a, x, slot, way))
        for a in "kv":
            arrived(("y2", a, x, slot))

    def swap_q(x):
        for d, peer in enumerate(others):
            begin = pl.multiple_of(peer * qwidth + x * wide, wide)
            send(
                ("q", x, d), rq_ref.at[:, pl.ds(begin, wide)],
                rqb.at[head, :, pl.ds(x * wide, wide)], {"head": peer},
            )

    def swap_kv():
        for d, peer in enumerate(others):
            begin = pl.multiple_of(peer * kv * HEAD_DIM, kv * HEAD_DIM)
            for name, src, dst in (("rk", rk_ref, rkb), ("rv", rv_ref, rvb)):
                send(
                    (name, d), src.at[:, pl.ds(begin, kv * HEAD_DIM)], dst.at[head],
                    {"head": peer},
                )

    def swap_out(x):
        to = pl.multiple_of(head * qwidth + x * wide, wide)
        for d, peer in enumerate(others):
            send(
                ("o", x, d), rob.at[peer, :, pl.ds(x * wide, wide)],
                ro_ref.at[:, pl.ds(to, wide)], {"head": peer},
            )
        bring(rob.at[head, :, pl.ds(x * wide, wide)], ro_ref.at[:, pl.ds(to, wide)])

    def attend(x, keys, values, begin, tile, count, first, visible):
        for i in range(count):
            here = pl.ds(begin + i * tile, tile)
            k, v = keys(), values()
            scores = lax.dot_general(
                qs[x, here, :], k, (((1,), (1,)), ((), ())), preferred_element_type=jnp.float32
            )
            if visible is not None:
                scores = jnp.where(visible(scores.shape), scores, very_low)
            high = jnp.max(scores, axis=1, keepdims=True)
            if first:
                high = jnp.broadcast_to(high, (tile, HEAD_DIM))
            else:
                before = top[x, here, :]
                high = jnp.maximum(before, high)
            top[x, here, :] = high
            count_keys = k.shape[0]
            spread = jnp.concatenate([high] * -(-count_keys // HEAD_DIM), axis=1)[:, :count_keys]
            weights = jnp.exp2((scores - spread) * SCALE).astype(jnp.bfloat16)
            both = jnp.concatenate([v, jnp.ones_like(v)], axis=1)
            mixed = jnp.dot(weights, both, preferred_element_type=jnp.float32)
            if not first:
                factor = jnp.exp2((before - high) * SCALE)
                mixed = acc[x, here, :] * jnp.concatenate([factor, factor], axis=1) + mixed
            acc[x, here, :] = mixed

    def block(buf, slot, x):
        return lambda: buf[slot, x]

    per = parts * toks
    resp_tile, prompt_tile = resp_rows, GROUP * rows

    def resp_slot(x, slot):
        attend(
            x, block(kbuf, slot, x), block(vbuf, slot, x), 0, resp_tile, resp_rows // resp_tile,
            False, None,
        )

    def resp_own(x):
        def flat(buf):
            return lambda: buf[:, :, x * HEAD_DIM : (x + 1) * HEAD_DIM].reshape(per, HEAD_DIM)

        def visible(shape):
            row = lax.rem(lax.broadcasted_iota(jnp.int32, shape, 0), per)
            return lax.broadcasted_iota(jnp.int32, shape, 1) <= row

        attend(x, flat(rkb), flat(rvb), 0, resp_tile, resp_rows // resp_tile, True, visible)

    def prompt_slot(x, slot):
        def visible(shape):
            row = lax.rem(lax.broadcasted_iota(jnp.int32, shape, 0), rows) + y * rows
            return lax.broadcasted_iota(jnp.int32, shape, 1) <= row

        def run():
            attend(
                x, block(kbuf, slot, x), block(vbuf, slot, x), resp_rows, prompt_tile, 1,
                slot == 0, visible if slot == 0 else None,
            )

        if slot == 0:
            run()
        else:
            pl.when({1: zh >= 1, 2: zh == RING - 1, 3: zh >= 2}[slot])(run)

    def stack_prompt():
        for x in range(kv):
            for g in range(GROUP):
                at_col = (x * GROUP + g) * HEAD_DIM
                qs[x, pl.ds(resp_rows + g * rows, rows), :] = pq[:, at_col : at_col + HEAD_DIM]

    def stack_resp(x):
        for g in range(GROUP):
            at_col = (x * GROUP + g) * HEAD_DIM
            qs[x, pl.ds(g * per, per), :] = rqb[:, :, at_col : at_col + HEAD_DIM].reshape(
                per, HEAD_DIM
            )

    def quotient(x, begin, count):
        part = acc[x, pl.ds(begin, count), :]
        return (part[:, :HEAD_DIM] / part[:, HEAD_DIM:]).astype(jnp.bfloat16)

    def finish_resp(x):
        for g in range(GROUP):
            at_col = (x * GROUP + g) * HEAD_DIM
            rob[:, :, at_col : at_col + HEAD_DIM] = quotient(x, g * per, per).reshape(
                parts, toks, HEAD_DIM
            )

    def finish_prompt(x):
        for g in range(GROUP):
            at_col = (x * GROUP + g) * HEAD_DIM
            pob[:, at_col : at_col + HEAD_DIM] = quotient(x, resp_rows + g * rows, rows)
        part = pl.ds(x * wide, wide)
        bring(pob.at[:, part], po_ref.at[:, part])

    def first_sends(x):
        z1("k", x, 1)
        z1("v", x, -1)
        z1("v", x, 1)
        z1("k", x, -1)
        y1("k", x, 0)
        y1("v", x, 0)

    def after_z1(x):
        arrived(("z1", "k", x, 1))
        z2("k", x)
        y1("k", x, 1)
        arrived(("z1", "v", x, -1))
        z2("v", x)
        y1("v", x, 2)
        arrived(("z1", "v", x, 1))
        y1("v", x, 1)
        arrived(("z1", "k", x, -1))
        y1("k", x, 2)

    def after_z2(x):
        for a in "kv":
            arrived(("z2", a, x))
            y1(a, x, 3)

    def take_resp(x):
        if x == 0:
            for d in range(parts - 1):
                arrived(("rk", d))
                arrived(("rv", d))
        for d in range(parts - 1):
            arrived(("q", x, d))
        stack_resp(x)

    for copy in got_kv:
        copy.wait()
    first_sends(0)
    first_sends(1)
    swap_q(0)
    swap_kv()
    swap_q(1)
    got_pq.wait()
    stack_prompt()
    for copy in got_resp:
        copy.wait()
    y2(0, 0)
    y2(1, 0)
    whole(0, 0)
    prompt_slot(0, 0)
    after_z1(0)
    whole(1, 0)
    prompt_slot(1, 0)
    after_z1(1)
    take_resp(0)
    resp_own(0)
    resp_slot(0, 0)
    y2(0, 1)
    y2(0, 2)
    take_resp(1)
    resp_own(1)
    resp_slot(1, 0)
    y2(1, 1)
    y2(1, 2)
    after_z2(0)
    whole(0, 1)
    resp_slot(0, 1)
    whole(0, 2)
    resp_slot(0, 2)
    after_z2(1)
    whole(1, 1)
    resp_slot(1, 1)
    whole(1, 2)
    resp_slot(1, 2)
    y2(0, 3)
    prompt_slot(0, 1)
    prompt_slot(0, 2)
    y2(1, 3)
    whole(0, 3)
    resp_slot(0, 3)
    finish_resp(0)
    swap_out(0)
    whole(1, 3)
    resp_slot(1, 3)
    finish_resp(1)
    swap_out(1)
    prompt_slot(0, 3)
    finish_prompt(0)
    prompt_slot(1, 1)
    prompt_slot(1, 2)
    prompt_slot(1, 3)
    finish_prompt(1)
    for x in range(kv):
        for d in range(parts - 1):
            arrived(("o", x, d))
    for copy in sent.values():
        copy.wait_send()
    for copy in local[1 + len(got_kv) + len(got_resp):]:
        copy.wait()


def on_device(prompt_q, prompt_k, prompt_v, resp_q, resp_k, resp_v, lengths):
    rows, qwidth = prompt_q.shape
    kwidth = prompt_k.shape[1]
    toks = resp_q.shape[1]
    parts = lax.axis_size("head")
    kv = kwidth // HEAD_DIM
    total = GROUP * (rows + parts * toks)
    any_place = pl.BlockSpec(memory_space=pltpu.HBM)
    bf16 = jnp.bfloat16
    messages = 80
    prompt_out, mixed = pl.pallas_call(
        functools.partial(kernel, (rows, toks, parts)),
        out_shape=(
            jax.ShapeDtypeStruct((rows, qwidth), bf16),
            jax.ShapeDtypeStruct((toks, parts * qwidth), bf16),
        ),
        in_specs=[any_place] * 6,
        out_specs=(any_place, any_place),
        scratch_shapes=[
            pltpu.VMEM((RING, kv, RING * rows, HEAD_DIM), bf16),
            pltpu.VMEM((RING, kv, RING * rows, HEAD_DIM), bf16),
            pltpu.VMEM((rows, qwidth), bf16),
            pltpu.VMEM((parts, toks, qwidth), bf16),
            pltpu.VMEM((parts, toks, kwidth), bf16),
            pltpu.VMEM((parts, toks, kwidth), bf16),
            pltpu.VMEM((kv, total, HEAD_DIM), bf16),
            pltpu.VMEM((kv, total, HEAD_DIM), jnp.float32),
            pltpu.VMEM((kv, total, 2 * HEAD_DIM), jnp.float32),
            pltpu.VMEM((rows, qwidth), bf16),
            pltpu.VMEM((parts, toks, qwidth), bf16),
            pltpu.SemaphoreType.DMA((messages,)),
            pltpu.SemaphoreType.DMA((messages,)),
            pltpu.SemaphoreType.DMA((16,)),
        ],
        compiler_params=pltpu.CompilerParams(
            collective_id=0, has_side_effects=True, vmem_limit_bytes=48 * 1024 * 1024
        ),
    )(prompt_q, prompt_k, prompt_v, resp_q[0], resp_k[0], resp_v[0])
    positions = lax.axis_index("head") * toks + jnp.arange(toks)
    live = positions < lengths[0]
    resp_out = jnp.where(live[:, None], mixed, jnp.zeros_like(mixed))[None]
    return (prompt_out, resp_out)


def solution(mesh):
    placed = (
        P(("grp", "seq"), "head"),
        P(("grp", "seq"), "head"),
        P(("grp", "seq"), "head"),
        P(("grp", "seq"), "head", None),
        P(("grp", "seq"), "head", None),
        P(("grp", "seq"), "head", None),
        P(("grp", "seq")),
    )
    return jax.shard_map(
        on_device,
        mesh=mesh,
        in_specs=placed,
        out_specs=(P(("grp", "seq"), "head"), P(("grp", "seq"), "head", None)),
        check_vma=False,
    )
```

```python
import functools
import math

import jax
import jax.numpy as jnp
from jax import lax
from jax.experimental import pallas as pl
from jax.experimental.pallas import tpu as pltpu
from jax.sharding import PartitionSpec as P

HEAD_DIM = 128
GROUP = 8
MESH = pl.DeviceIdType.MESH
SCALE = math.log2(math.e) / math.sqrt(HEAD_DIM)
very_low = -1e30

RING = 4


def kernel(
    sizes,
    pq_ref, pk_ref, pv_ref, rq_ref, rk_ref, rv_ref,
    po_ref, ro_ref,
    kbuf, vbuf, pq, rqb, rkb, rvb, qs, top, acc, pob, rob,
    send_sem, recv_sem, local_sem,
):
    rows, toks, parts = sizes
    kv = 2
    wide = GROUP * HEAD_DIM
    qwidth = kv * wide
    resp_rows = GROUP * parts * toks
    chunk = RING * rows

    seq = lax.axis_index("seq")
    head = lax.axis_index("head")
    zh, y = seq // RING, lax.rem(seq, RING)

    def at(dz, dy):
        return lax.rem(zh + dz + RING, RING) * RING + lax.rem(y + dy + RING, RING)

    z_next, z_prev = at(1, 0), at(-1, 0)
    y_next, y_prev = at(0, 1), at(0, -1)
    others = [lax.rem(head + d, parts) for d in range(1, parts)]

    barrier = pltpu.get_barrier_semaphore()
    for peer in (z_next, z_prev, y_next, y_prev):
        pl.semaphore_signal(barrier, inc=1, device_id={"seq": peer}, device_id_type=MESH)
    for peer in others:
        pl.semaphore_signal(barrier, inc=1, device_id={"head": peer}, device_id_type=MESH)

    def rows_of(dy):
        return pl.ds(pl.multiple_of(lax.rem(y + dy + RING, RING) * rows, 16), rows)

    mine = rows_of(0)
    bufs, given = {"k": kbuf, "v": vbuf}, {"k": pk_ref, "v": pv_ref}

    local = []

    def bring(src, dst):
        copy = pltpu.make_async_copy(src, dst, local_sem.at[len(local)])
        copy.start()
        local.append(copy)
        return copy

    got_pq = bring(pq_ref, pq)
    got_kv = [
        bring(given[a].at[:, pl.ds(x * HEAD_DIM, HEAD_DIM)], bufs[a].at[0, x, mine])
        for x in range(kv)
        for a in "kv"
    ]
    own_q = pl.ds(pl.multiple_of(head * qwidth, qwidth), qwidth)
    own_kv = pl.ds(pl.multiple_of(head * kv * HEAD_DIM, kv * HEAD_DIM), kv * HEAD_DIM)
    got_resp = [
        bring(rq_ref.at[:, own_q], rqb.at[head]),
        bring(rk_ref.at[:, own_kv], rkb.at[head]),
        bring(rv_ref.at[:, own_kv], rvb.at[head]),
    ]
    pl.semaphore_wait(barrier, 4 + len(others))

    sent = {}

    def send(name, src, dst, peer):
        copy = pltpu.make_async_remote_copy(
            src_ref=src,
            dst_ref=dst,
            send_sem=send_sem.at[len(sent)],
            recv_sem=recv_sem.at[len(sent)],
            device_id=peer,
            device_id_type=MESH,
        )
        copy.start()
        sent[name] = copy

    def arrived(name):
        sent[name].wait_recv()

    def z1(a, x, way):
        slot = 1 if way > 0 else 2
        send(
            ("z1", a, x, way), bufs[a].at[0, x, mine], bufs[a].at[slot, x, mine],
            {"seq": z_next if way > 0 else z_prev},
        )

    def z2(a, x):
        slot, peer = (1, z_next) if a == "k" else (2, z_prev)
        send(
            ("z2", a, x), bufs[a].at[slot, x, mine], bufs[a].at[3, x, mine],
            {"seq": peer},
        )

    def y1(a, x, slot):
        place = bufs[a].at[slot, x, mine]
        for way in (1, -1) if a == "k" else (-1, 1):
            send(("y1", a, x, slot, way), place, place, {"seq": y_next if way > 0 else y_prev})

    def y2(a, x, slot):
        way = 1 if a == "k" else -1
        arrived(("y1", a, x, slot, way))
        place = bufs[a].at[slot, x, rows_of(-way)]
        send(("y2", a, x, slot), place, place, {"seq": y_next if way > 0 else y_prev})

    def whole(x, slot):
        for a, way in (("k", -1), ("v", 1)):
            arrived(("y1", a, x, slot, way))
        for a in "kv":
            arrived(("y2", a, x, slot))

    def swap_q(x):
        for d, peer in enumerate(others):
            begin = pl.multiple_of(peer * qwidth + x * wide, wide)
            send(
                ("q", x, d), rq_ref.at[:, pl.ds(begin, wide)],
                rqb.at[head, :, pl.ds(x * wide, wide)], {"head": peer},
            )

    def swap_kv():
        for d, peer in enumerate(others):
            begin = pl.multiple_of(peer * kv * HEAD_DIM, kv * HEAD_DIM)
            for name, src, dst in (("rk", rk_ref, rkb), ("rv", rv_ref, rvb)):
                send(
                    (name, d), src.at[:, pl.ds(begin, kv * HEAD_DIM)], dst.at[head],
                    {"head": peer},
                )

    def swap_out(x):
        to = pl.multiple_of(head * qwidth + x * wide, wide)
        for d, peer in enumerate(others):
            send(
                ("o", x, d), rob.at[peer, :, pl.ds(x * wide, wide)],
                ro_ref.at[:, pl.ds(to, wide)], {"head": peer},
            )
        bring(rob.at[head, :, pl.ds(x * wide, wide)], ro_ref.at[:, pl.ds(to, wide)])

    def attend(x, keys, values, begin, tile, count, first, visible):
        for i in range(count):
            here = pl.ds(begin + i * tile, tile)
            k, v = keys(), values()
            scores = lax.dot_general(
                qs[x, here, :], k, (((1,), (1,)), ((), ())), preferred_element_type=jnp.float32
            )
            if visible is not None:
                scores = jnp.where(visible(scores.shape), scores, very_low)
            high = jnp.max(scores, axis=1, keepdims=True)
            if first:
                high = jnp.broadcast_to(high, (tile, HEAD_DIM))
            else:
                before = top[x, here, :]
                high = jnp.maximum(before, high)
            top[x, here, :] = high
            count_keys = k.shape[0]
            spread = jnp.concatenate([high] * -(-count_keys // HEAD_DIM), axis=1)[:, :count_keys]
            weights = jnp.exp2((scores - spread) * SCALE).astype(jnp.bfloat16)
            both = jnp.concatenate([v, jnp.ones_like(v)], axis=1)
            mixed = jnp.dot(weights, both, preferred_element_type=jnp.float32)
            if not first:
                factor = jnp.exp2((before - high) * SCALE)
                mixed = acc[x, here, :] * jnp.concatenate([factor, factor], axis=1) + mixed
            acc[x, here, :] = mixed

    def block(buf, slot, x):
        return lambda: buf[slot, x]

    per = parts * toks
    resp_tile, prompt_tile = resp_rows, GROUP * rows

    def resp_slot(x, slot):
        attend(
            x, block(kbuf, slot, x), block(vbuf, slot, x), 0, resp_tile, resp_rows // resp_tile,
            False, None,
        )

    def resp_own(x):
        def flat(buf):
            return lambda: buf[:, :, x * HEAD_DIM : (x + 1) * HEAD_DIM].reshape(per, HEAD_DIM)

        def visible(shape):
            row = lax.rem(lax.broadcasted_iota(jnp.int32, shape, 0), per)
            return lax.broadcasted_iota(jnp.int32, shape, 1) <= row

        attend(x, flat(rkb), flat(rvb), 0, resp_tile, resp_rows // resp_tile, True, visible)

    def prompt_slot(x, slot):
        def visible(shape):
            row = lax.rem(lax.broadcasted_iota(jnp.int32, shape, 0), rows) + y * rows
            return lax.broadcasted_iota(jnp.int32, shape, 1) <= row

        def run():
            attend(
                x, block(kbuf, slot, x), block(vbuf, slot, x), resp_rows, prompt_tile, 1,
                slot == 0, visible if slot == 0 else None,
            )

        if slot == 0:
            run()
        else:
            pl.when({1: zh >= 1, 2: zh == RING - 1, 3: zh >= 2}[slot])(run)

    def stack_prompt():
        for x in range(kv):
            for g in range(GROUP):
                at_col = (x * GROUP + g) * HEAD_DIM
                qs[x, pl.ds(resp_rows + g * rows, rows), :] = pq[:, at_col : at_col + HEAD_DIM]

    def stack_resp(x):
        for g in range(GROUP):
            at_col = (x * GROUP + g) * HEAD_DIM
            qs[x, pl.ds(g * per, per), :] = rqb[:, :, at_col : at_col + HEAD_DIM].reshape(
                per, HEAD_DIM
            )

    def quotient(x, begin, count):
        part = acc[x, pl.ds(begin, count), :]
        return (part[:, :HEAD_DIM] / part[:, HEAD_DIM:]).astype(jnp.bfloat16)

    def finish_resp(x):
        for g in range(GROUP):
            at_col = (x * GROUP + g) * HEAD_DIM
            rob[:, :, at_col : at_col + HEAD_DIM] = quotient(x, g * per, per).reshape(
                parts, toks, HEAD_DIM
            )

    def finish_prompt(x):
        for g in range(GROUP):
            at_col = (x * GROUP + g) * HEAD_DIM
            pob[:, at_col : at_col + HEAD_DIM] = quotient(x, resp_rows + g * rows, rows)
        part = pl.ds(x * wide, wide)
        bring(pob.at[:, part], po_ref.at[:, part])

    left = set()

    def gone(name):
        if name not in left:
            left.add(name)
            sent[name].wait_send()

    def first_z(pairs):
        for x in range(kv):
            for a, way in pairs:
                z1(a, x, way)

    def first_y():
        for x in range(kv):
            y1("k", x, 0)
            y1("v", x, 0)

    def pass_on(x):
        for a, slot, way in (("k", 1, 1), ("v", 2, -1)):
            arrived(("z1", a, x, way))
            z2(a, x)
            y1(a, x, slot)

    def spread(x):
        for a, slot, way in (("v", 1, 1), ("k", 2, -1)):
            arrived(("z1", a, x, way))
            y1(a, x, slot)

    def after_z2(x):
        for a in "kv":
            arrived(("z2", a, x))
            y1(a, x, 3)

    def take_resp(x):
        if x == 0:
            for d in range(parts - 1):
                arrived(("rk", d))
                arrived(("rv", d))
        for d in range(parts - 1):
            arrived(("q", x, d))
        stack_resp(x)

    onward = (("k", 1), ("v", -1))
    rest = (("v", 1), ("k", -1))
    for copy in got_kv:
        copy.wait()
    first_z(onward)
    first_y()
    first_z(rest)
    got_pq.wait()
    stack_prompt()
    for copy in got_resp:
        copy.wait()
    for x in range(kv):
        y2("k", x, 0)
        y2("v", x, 0)
    pass_on(0)
    whole(0, 0)
    prompt_slot(0, 0)
    pass_on(1)
    whole(1, 0)
    swap_kv()
    swap_q(0)
    swap_q(1)
    prompt_slot(1, 0)
    y2("k", 0, 1)
    y2("v", 0, 2)
    spread(0)
    y2("k", 1, 1)
    y2("v", 1, 2)
    spread(1)
    y2("v", 0, 1)
    y2("k", 0, 2)
    after_z2(0)
    y2("v", 1, 1)
    y2("k", 1, 2)
    after_z2(1)
    whole(0, 1)
    prompt_slot(0, 1)
    y2("k", 0, 3)
    y2("v", 0, 3)
    whole(0, 2)
    prompt_slot(0, 2)
    take_resp(0)
    resp_own(0)
    resp_slot(0, 0)
    y2("k", 1, 3)
    y2("v", 1, 3)
    resp_slot(0, 1)
    resp_slot(0, 2)
    take_resp(1)
    resp_own(1)
    resp_slot(1, 0)
    whole(1, 1)
    resp_slot(1, 1)
    whole(1, 2)
    resp_slot(1, 2)
    whole(0, 3)
    resp_slot(0, 3)
    finish_resp(0)
    swap_out(0)
    whole(1, 3)
    resp_slot(1, 3)
    finish_resp(1)
    swap_out(1)
    prompt_slot(0, 3)
    finish_prompt(0)
    prompt_slot(1, 1)
    prompt_slot(1, 2)
    prompt_slot(1, 3)
    finish_prompt(1)
    for x in range(kv):
        for d in range(parts - 1):
            arrived(("o", x, d))
    for name in sent:
        gone(name)
    for copy in local[1 + len(got_kv) + len(got_resp):]:
        copy.wait()


def on_device(prompt_q, prompt_k, prompt_v, resp_q, resp_k, resp_v, lengths):
    rows, qwidth = prompt_q.shape
    kwidth = prompt_k.shape[1]
    toks = resp_q.shape[1]
    parts = lax.axis_size("head")
    kv = kwidth // HEAD_DIM
    total = GROUP * (rows + parts * toks)
    any_place = pl.BlockSpec(memory_space=pltpu.HBM)
    bf16 = jnp.bfloat16
    messages = 80
    prompt_out, mixed = pl.pallas_call(
        functools.partial(kernel, (rows, toks, parts)),
        out_shape=(
            pltpu.VMEM((rows, qwidth), bf16),
            pltpu.VMEM((toks, parts * qwidth), bf16),
        ),
        in_specs=[any_place] * 6,
        out_specs=(any_place, any_place),
        scratch_shapes=[
            pltpu.VMEM((RING, kv, RING * rows, HEAD_DIM), bf16),
            pltpu.VMEM((RING, kv, RING * rows, HEAD_DIM), bf16),
            pltpu.VMEM((rows, qwidth), bf16),
            pltpu.VMEM((parts, toks, qwidth), bf16),
            pltpu.VMEM((parts, toks, kwidth), bf16),
            pltpu.VMEM((parts, toks, kwidth), bf16),
            pltpu.VMEM((kv, total, HEAD_DIM), bf16),
            pltpu.VMEM((kv, total, HEAD_DIM), jnp.float32),
            pltpu.VMEM((kv, total, 2 * HEAD_DIM), jnp.float32),
            pltpu.VMEM((rows, qwidth), bf16),
            pltpu.VMEM((parts, toks, qwidth), bf16),
            pltpu.SemaphoreType.DMA((messages,)),
            pltpu.SemaphoreType.DMA((messages,)),
            pltpu.SemaphoreType.DMA((16,)),
        ],
        compiler_params=pltpu.CompilerParams(
            collective_id=0, has_side_effects=True, vmem_limit_bytes=60 * 1024 * 1024
        ),
    )(prompt_q, prompt_k, prompt_v, resp_q[0], resp_k[0], resp_v[0])
    positions = lax.axis_index("head") * toks + jnp.arange(toks)
    live = positions < lengths[0]
    resp_out = jnp.where(live[:, None], mixed, jnp.zeros_like(mixed))[None]
    return (prompt_out, resp_out)


def solution(mesh):
    placed = (
        P(("grp", "seq"), "head"),
        P(("grp", "seq"), "head"),
        P(("grp", "seq"), "head"),
        P(("grp", "seq"), "head", None),
        P(("grp", "seq"), "head", None),
        P(("grp", "seq"), "head", None),
        P(("grp", "seq")),
    )
    return jax.shard_map(
        on_device,
        mesh=mesh,
        in_specs=placed,
        out_specs=(P(("grp", "seq"), "head"), P(("grp", "seq"), "head", None)),
        check_vma=False,
    )
```

```python
import functools
import math

import jax
import jax.numpy as jnp
from jax import lax
from jax.experimental import pallas as pl
from jax.experimental.pallas import tpu as pltpu
from jax.sharding import PartitionSpec as P

HEAD_DIM = 128
GROUP = 8
MESH = pl.DeviceIdType.MESH
SCALE = math.log2(math.e) / math.sqrt(HEAD_DIM)
very_low = -1e30

RING = 4


def kernel(
    sizes,
    pq_ref, pk_ref, pv_ref, rq_ref, rk_ref, rv_ref,
    po_ref, ro_ref,
    kbuf, vbuf, pq, rqb, rkb, rvb, qs, top, acc, pob, rob,
    send_sem, recv_sem, local_sem,
):
    rows, toks, parts = sizes
    kv = 2
    wide = GROUP * HEAD_DIM
    qwidth = kv * wide
    resp_rows = GROUP * parts * toks
    chunk = RING * rows

    seq = lax.axis_index("seq")
    head = lax.axis_index("head")
    zh, y = seq // RING, lax.rem(seq, RING)

    def at(dz, dy):
        return lax.rem(zh + dz + RING, RING) * RING + lax.rem(y + dy + RING, RING)

    z_next, z_prev = at(1, 0), at(-1, 0)
    y_next, y_prev = at(0, 1), at(0, -1)
    others = [lax.rem(head + d, parts) for d in range(1, parts)]

    barrier = pltpu.get_barrier_semaphore()
    for peer in (z_next, z_prev, y_next, y_prev, at(0, 2)):
        pl.semaphore_signal(barrier, inc=1, device_id={"seq": peer}, device_id_type=MESH)
    for peer in others:
        pl.semaphore_signal(barrier, inc=1, device_id={"head": peer}, device_id_type=MESH)

    def rows_of(dy):
        return pl.ds(pl.multiple_of(lax.rem(y + dy + RING, RING) * rows, 16), rows)

    mine = rows_of(0)
    bufs, given = {"k": kbuf, "v": vbuf}, {"k": pk_ref, "v": pv_ref}

    local = []

    def bring(src, dst):
        copy = pltpu.make_async_copy(src, dst, local_sem.at[len(local)])
        copy.start()
        local.append(copy)
        return copy

    got_pq = bring(pq_ref, pq)
    got_kv = [
        bring(given[a].at[:, pl.ds(x * HEAD_DIM, HEAD_DIM)], bufs[a].at[0, x, mine])
        for x in range(kv)
        for a in "kv"
    ]
    own_q = pl.ds(pl.multiple_of(head * qwidth, qwidth), qwidth)
    own_kv = pl.ds(pl.multiple_of(head * kv * HEAD_DIM, kv * HEAD_DIM), kv * HEAD_DIM)
    got_resp = [
        bring(rq_ref.at[:, own_q], rqb.at[head]),
        bring(rk_ref.at[:, own_kv], rkb.at[head]),
        bring(rv_ref.at[:, own_kv], rvb.at[head]),
    ]
    pl.semaphore_wait(barrier, 5 + len(others))

    straight = (0, 1, 2, 3)
    sent = {}

    def send(name, src, dst, peer):
        copy = pltpu.make_async_remote_copy(
            src_ref=src,
            dst_ref=dst,
            send_sem=send_sem.at[len(sent)],
            recv_sem=recv_sem.at[len(sent)],
            device_id=peer,
            device_id_type=MESH,
        )
        copy.start()
        sent[name] = copy

    def arrived(name):
        sent[name].wait_recv()

    def z1(a, x, way):
        slot = 1 if way > 0 else 2
        send(
            ("z1", a, x, way), bufs[a].at[0, x, mine], bufs[a].at[slot, x, mine],
            {"seq": z_next if way > 0 else z_prev},
        )

    def z2(a, x):
        slot, peer = (1, z_next) if a == "k" else (2, z_prev)
        send(
            ("z2", a, x), bufs[a].at[slot, x, mine], bufs[a].at[3, x, mine],
            {"seq": peer},
        )

    def y1(a, x, slot):
        place = bufs[a].at[slot, x, mine]
        ways = (1, -1) if a == "k" else (-1, 1)
        for way in ways + ((2,) if slot in straight else ()):
            send(("y1", a, x, slot, way), place, place, {"seq": at(0, way)})

    def y2(a, x, slot):
        if slot in straight:
            return
        way = 1 if a == "k" else -1
        arrived(("y1", a, x, slot, way))
        place = bufs[a].at[slot, x, rows_of(-way)]
        send(("y2", a, x, slot), place, place, {"seq": y_next if way > 0 else y_prev})

    def whole(x, slot):
        for a, way in (("k", -1), ("v", 1)):
            if slot in straight:
                arrived(("y1", a, x, slot, -way))
            arrived(("y1", a, x, slot, way))
            arrived(("y1", a, x, slot, 2) if slot in straight else ("y2", a, x, slot))

    def swap_q(x):
        for d, peer in enumerate(others):
            begin = pl.multiple_of(peer * qwidth + x * wide, wide)
            send(
                ("q", x, d), rq_ref.at[:, pl.ds(begin, wide)],
                rqb.at[head, :, pl.ds(x * wide, wide)], {"head": peer},
            )

    def swap_kv():
        for d, peer in enumerate(others):
            begin = pl.multiple_of(peer * kv * HEAD_DIM, kv * HEAD_DIM)
            for name, src, dst in (("rk", rk_ref, rkb), ("rv", rv_ref, rvb)):
                send(
                    (name, d), src.at[:, pl.ds(begin, kv * HEAD_DIM)], dst.at[head],
                    {"head": peer},
                )

    def swap_out(x):
        to = pl.multiple_of(head * qwidth + x * wide, wide)
        for d, peer in enumerate(others):
            send(
                ("o", x, d), rob.at[peer, :, pl.ds(x * wide, wide)],
                ro_ref.at[:, pl.ds(to, wide)], {"head": peer},
            )
        bring(rob.at[head, :, pl.ds(x * wide, wide)], ro_ref.at[:, pl.ds(to, wide)])

    def attend(x, keys, values, begin, tile, count, first, visible):
        for i in range(count):
            here = pl.ds(begin + i * tile, tile)
            k, v = keys(), values()
            scores = lax.dot_general(
                qs[x, here, :], k, (((1,), (1,)), ((), ())), preferred_element_type=jnp.float32
            )
            if visible is not None:
                scores = jnp.where(visible(scores.shape), scores, very_low)
            high = jnp.max(scores, axis=1, keepdims=True)
            if first:
                high = jnp.broadcast_to(high, (tile, HEAD_DIM))
            else:
                before = top[x, here, :]
                high = jnp.maximum(before, high)
            top[x, here, :] = high
            count_keys = k.shape[0]
            spread = jnp.concatenate([high] * -(-count_keys // HEAD_DIM), axis=1)[:, :count_keys]
            weights = jnp.exp2((scores - spread) * SCALE).astype(jnp.bfloat16)
            both = jnp.concatenate([v, jnp.ones_like(v)], axis=1)
            mixed = jnp.dot(weights, both, preferred_element_type=jnp.float32)
            if not first:
                factor = jnp.exp2((before - high) * SCALE)
                mixed = acc[x, here, :] * jnp.concatenate([factor, factor], axis=1) + mixed
            acc[x, here, :] = mixed

    def block(buf, slot, x):
        return lambda: buf[slot, x]

    per = parts * toks
    resp_tile, prompt_tile = resp_rows, GROUP * rows

    def resp_slot(x, slot):
        attend(
            x, block(kbuf, slot, x), block(vbuf, slot, x), 0, resp_tile, resp_rows // resp_tile,
            False, None,
        )

    def resp_own(x):
        def flat(buf):
            return lambda: buf[:, :, x * HEAD_DIM : (x + 1) * HEAD_DIM].reshape(per, HEAD_DIM)

        def visible(shape):
            row = lax.rem(lax.broadcasted_iota(jnp.int32, shape, 0), per)
            return lax.broadcasted_iota(jnp.int32, shape, 1) <= row

        attend(x, flat(rkb), flat(rvb), 0, resp_tile, resp_rows // resp_tile, True, visible)

    def prompt_slot(x, slot):
        def visible(shape):
            row = lax.rem(lax.broadcasted_iota(jnp.int32, shape, 0), rows) + y * rows
            return lax.broadcasted_iota(jnp.int32, shape, 1) <= row

        def run():
            attend(
                x, block(kbuf, slot, x), block(vbuf, slot, x), resp_rows, prompt_tile, 1,
                slot == 0, visible if slot == 0 else None,
            )

        if slot == 0:
            run()
        else:
            pl.when({1: zh >= 1, 2: zh == RING - 1, 3: zh >= 2}[slot])(run)

    def stack_prompt():
        for x in range(kv):
            for g in range(GROUP):
                at_col = (x * GROUP + g) * HEAD_DIM
                qs[x, pl.ds(resp_rows + g * rows, rows), :] = pq[:, at_col : at_col + HEAD_DIM]

    def stack_resp(x):
        for g in range(GROUP):
            at_col = (x * GROUP + g) * HEAD_DIM
            qs[x, pl.ds(g * per, per), :] = rqb[:, :, at_col : at_col + HEAD_DIM].reshape(
                per, HEAD_DIM
            )

    def quotient(x, begin, count):
        part = acc[x, pl.ds(begin, count), :]
        return (part[:, :HEAD_DIM] / part[:, HEAD_DIM:]).astype(jnp.bfloat16)

    def finish_resp(x):
        for g in range(GROUP):
            at_col = (x * GROUP + g) * HEAD_DIM
            rob[:, :, at_col : at_col + HEAD_DIM] = quotient(x, g * per, per).reshape(
                parts, toks, HEAD_DIM
            )

    def finish_prompt(x):
        for g in range(GROUP):
            at_col = (x * GROUP + g) * HEAD_DIM
            pob[:, at_col : at_col + HEAD_DIM] = quotient(x, resp_rows + g * rows, rows)
        part = pl.ds(x * wide, wide)
        bring(pob.at[:, part], po_ref.at[:, part])

    left = set()

    def gone(name):
        if name not in left:
            left.add(name)
            sent[name].wait_send()

    def first_z(pairs):
        for x in range(kv):
            for a, way in pairs:
                z1(a, x, way)

    def first_y():
        for x in range(kv):
            y1("k", x, 0)
            y1("v", x, 0)

    def pass_on(x):
        for a, slot, way in (("k", 1, 1), ("v", 2, -1)):
            arrived(("z1", a, x, way))
            z2(a, x)
            y1(a, x, slot)

    def spread(x):
        for a, slot, way in (("v", 1, 1), ("k", 2, -1)):
            arrived(("z1", a, x, way))
            y1(a, x, slot)

    def after_z2(x):
        for a in "kv":
            arrived(("z2", a, x))
            y1(a, x, 3)

    def take_resp(x):
        if x == 0:
            for d in range(parts - 1):
                arrived(("rk", d))
                arrived(("rv", d))
        for d in range(parts - 1):
            arrived(("q", x, d))
        stack_resp(x)

    onward = (("k", 1), ("v", -1))
    rest = (("v", 1), ("k", -1))
    for copy in got_kv:
        copy.wait()
    first_z(onward)
    first_y()
    first_z(rest)
    got_pq.wait()
    stack_prompt()
    for copy in got_resp:
        copy.wait()
    for x in range(kv):
        y2("k", x, 0)
        y2("v", x, 0)
    pass_on(0)
    whole(0, 0)
    prompt_slot(0, 0)
    pass_on(1)
    whole(1, 0)
    swap_kv()
    swap_q(0)
    swap_q(1)
    prompt_slot(1, 0)
    y2("k", 0, 1)
    y2("v", 0, 2)
    spread(0)
    y2("k", 1, 1)
    y2("v", 1, 2)
    spread(1)
    y2("v", 0, 1)
    y2("k", 0, 2)
    after_z2(0)
    y2("v", 1, 1)
    y2("k", 1, 2)
    after_z2(1)
    whole(0, 1)
    prompt_slot(0, 1)
    y2("k", 0, 3)
    y2("v", 0, 3)
    whole(0, 2)
    prompt_slot(0, 2)
    take_resp(0)
    resp_own(0)
    resp_slot(0, 0)
    y2("k", 1, 3)
    y2("v", 1, 3)
    resp_slot(0, 1)
    resp_slot(0, 2)
    take_resp(1)
    resp_own(1)
    resp_slot(1, 0)
    whole(1, 1)
    resp_slot(1, 1)
    whole(1, 2)
    resp_slot(1, 2)
    whole(0, 3)
    resp_slot(0, 3)
    finish_resp(0)
    swap_out(0)
    whole(1, 3)
    resp_slot(1, 3)
    finish_resp(1)
    swap_out(1)
    prompt_slot(0, 3)
    finish_prompt(0)
    prompt_slot(1, 1)
    prompt_slot(1, 2)
    prompt_slot(1, 3)
    finish_prompt(1)
    for x in range(kv):
        for d in range(parts - 1):
            arrived(("o", x, d))
    for name in sent:
        gone(name)
    for copy in local[1 + len(got_kv) + len(got_resp):]:
        copy.wait()


def on_device(prompt_q, prompt_k, prompt_v, resp_q, resp_k, resp_v, lengths):
    rows, qwidth = prompt_q.shape
    kwidth = prompt_k.shape[1]
    toks = resp_q.shape[1]
    parts = lax.axis_size("head")
    kv = kwidth // HEAD_DIM
    total = GROUP * (rows + parts * toks)
    any_place = pl.BlockSpec(memory_space=pltpu.HBM)
    bf16 = jnp.bfloat16
    messages = 88
    prompt_out, mixed = pl.pallas_call(
        functools.partial(kernel, (rows, toks, parts)),
        out_shape=(
            pltpu.VMEM((rows, qwidth), bf16),
            pltpu.VMEM((toks, parts * qwidth), bf16),
        ),
        in_specs=[any_place] * 6,
        out_specs=(any_place, any_place),
        scratch_shapes=[
            pltpu.VMEM((RING, kv, RING * rows, HEAD_DIM), bf16),
            pltpu.VMEM((RING, kv, RING * rows, HEAD_DIM), bf16),
            pltpu.VMEM((rows, qwidth), bf16),
            pltpu.VMEM((parts, toks, qwidth), bf16),
            pltpu.VMEM((parts, toks, kwidth), bf16),
            pltpu.VMEM((parts, toks, kwidth), bf16),
            pltpu.VMEM((kv, total, HEAD_DIM), bf16),
            pltpu.VMEM((kv, total, HEAD_DIM), jnp.float32),
            pltpu.VMEM((kv, total, 2 * HEAD_DIM), jnp.float32),
            pltpu.VMEM((rows, qwidth), bf16),
            pltpu.VMEM((parts, toks, qwidth), bf16),
            pltpu.SemaphoreType.DMA((messages,)),
            pltpu.SemaphoreType.DMA((messages,)),
            pltpu.SemaphoreType.DMA((16,)),
        ],
        compiler_params=pltpu.CompilerParams(
            collective_id=0, has_side_effects=True, vmem_limit_bytes=60 * 1024 * 1024
        ),
    )(prompt_q, prompt_k, prompt_v, resp_q[0], resp_k[0], resp_v[0])
    positions = lax.axis_index("head") * toks + jnp.arange(toks)
    live = positions < lengths[0]
    resp_out = jnp.where(live[:, None], mixed, jnp.zeros_like(mixed))[None]
    return (prompt_out, resp_out)


def solution(mesh):
    placed = (
        P(("grp", "seq"), "head"),
        P(("grp", "seq"), "head"),
        P(("grp", "seq"), "head"),
        P(("grp", "seq"), "head", None),
        P(("grp", "seq"), "head", None),
        P(("grp", "seq"), "head", None),
        P(("grp", "seq")),
    )
    return jax.shard_map(
        on_device,
        mesh=mesh,
        in_specs=placed,
        out_specs=(P(("grp", "seq"), "head"), P(("grp", "seq"), "head", None)),
        check_vma=False,
    )
```

```python
import functools
import math

import jax
import jax.numpy as jnp
from jax import lax
from jax.experimental import pallas as pl
from jax.experimental.pallas import tpu as pltpu
from jax.sharding import PartitionSpec as P

HEAD_DIM = 128
GROUP = 8
MESH = pl.DeviceIdType.MESH
SCALE = math.log2(math.e) / math.sqrt(HEAD_DIM)
very_low = -1e30

RING = 4


def kernel(
    sizes,
    pq_ref, pk_ref, pv_ref, rq_ref, rk_ref, rv_ref,
    po_ref, ro_ref,
    kbuf, vbuf, pq, rqb, rkb, rvb, qs, top, acc, pob, rob,
    send_sem, recv_sem, local_sem,
):
    rows, toks, parts = sizes
    kv = 2
    wide = GROUP * HEAD_DIM
    qwidth = kv * wide
    resp_rows = GROUP * parts * toks
    chunk = RING * rows

    seq = lax.axis_index("seq")
    head = lax.axis_index("head")
    zh, y = seq // RING, lax.rem(seq, RING)

    def at(dz, dy):
        return lax.rem(zh + dz + RING, RING) * RING + lax.rem(y + dy + RING, RING)

    z_next, z_prev = at(1, 0), at(-1, 0)
    y_next, y_prev = at(0, 1), at(0, -1)
    others = [lax.rem(head + d, parts) for d in range(1, parts)]

    along_z = {1: z_next, -1: z_prev}

    barrier = pltpu.get_barrier_semaphore()
    for peer in (z_next, z_prev, y_next, y_prev, at(0, 2)):
        pl.semaphore_signal(barrier, inc=1, device_id={"seq": peer}, device_id_type=MESH)
    for peer in others:
        pl.semaphore_signal(barrier, inc=1, device_id={"head": peer}, device_id_type=MESH)

    def rows_of(dy):
        return pl.ds(pl.multiple_of(lax.rem(y + dy + RING, RING) * rows, 16), rows)

    mine = rows_of(0)
    bufs, given = {"k": kbuf, "v": vbuf}, {"k": pk_ref, "v": pv_ref}

    local = []

    def bring(src, dst):
        copy = pltpu.make_async_copy(src, dst, local_sem.at[len(local)])
        copy.start()
        local.append(copy)
        return copy

    got_pq = bring(pq_ref, pq)
    got_kv = [
        bring(given[a].at[:, pl.ds(x * HEAD_DIM, HEAD_DIM)], bufs[a].at[0, x, mine])
        for x in range(kv)
        for a in "kv"
    ]
    own_q = pl.ds(pl.multiple_of(head * qwidth, qwidth), qwidth)
    own_kv = pl.ds(pl.multiple_of(head * kv * HEAD_DIM, kv * HEAD_DIM), kv * HEAD_DIM)
    got_resp = [
        bring(rq_ref.at[:, own_q], rqb.at[head]),
        bring(rk_ref.at[:, own_kv], rkb.at[head]),
        bring(rv_ref.at[:, own_kv], rvb.at[head]),
    ]
    pl.semaphore_wait(barrier, 5 + len(others))

    number = {}

    def message(name):
        kind, *which = name
        if kind == "z1":
            a, x, way = which
            src, dst = bufs[a].at[0, x, mine], bufs[a].at[1 if way > 0 else 2, x, mine]
            peer = {"seq": along_z[way]}
        elif kind == "z2":
            a, x = which
            slot, way = (1, 1) if a == "k" else (2, -1)
            src, dst = bufs[a].at[slot, x, mine], bufs[a].at[3, x, mine]
            peer = {"seq": along_z[way]}
        elif kind == "y":
            a, x, slot, way = which
            src = dst = bufs[a].at[slot, x, mine]
            peer = {"seq": at(0, way)}
        else:
            *x, d = which
            peer = {"head": others[d]}
            if kind == "q":
                begin = pl.multiple_of(others[d] * qwidth + x[0] * wide, wide)
                src = rq_ref.at[:, pl.ds(begin, wide)]
                dst = rqb.at[head, :, pl.ds(x[0] * wide, wide)]
            elif kind == "o":
                to = pl.multiple_of(head * qwidth + x[0] * wide, wide)
                src = rob.at[others[d], :, pl.ds(x[0] * wide, wide)]
                dst = ro_ref.at[:, pl.ds(to, wide)]
            else:
                begin = pl.multiple_of(others[d] * kv * HEAD_DIM, kv * HEAD_DIM)
                given, held = (rk_ref, rkb) if kind == "rk" else (rv_ref, rvb)
                src, dst = given.at[:, pl.ds(begin, kv * HEAD_DIM)], held.at[head]
        at_sem = number.setdefault(name, len(number))
        return pltpu.make_async_remote_copy(
            src_ref=src,
            dst_ref=dst,
            send_sem=send_sem.at[at_sem],
            recv_sem=recv_sem.at[at_sem],
            device_id=peer,
            device_id_type=MESH,
        )

    def send(*name):
        message(name).start()

    def arrived(*name):
        message(name).wait_recv()

    def y1(a, x, slot):
        for way in (1, -1, 2) if a == "k" else (-1, 1, 2):
            send("y", a, x, slot, way)

    def whole(x, slot):
        for way in (1, -1, 2):
            for a in "kv":
                arrived("y", a, x, slot, way)

    def swap_q(x):
        for d in range(parts - 1):
            send("q", x, d)

    def swap_kv():
        for d in range(parts - 1):
            send("rk", d)
            send("rv", d)

    def swap_out(x):
        for d in range(parts - 1):
            send("o", x, d)
        to = pl.multiple_of(head * qwidth + x * wide, wide)
        bring(rob.at[head, :, pl.ds(x * wide, wide)], ro_ref.at[:, pl.ds(to, wide)])

    def attend(x, keys, values, begin, tile, count, first, visible):
        for i in range(count):
            here = pl.ds(begin + i * tile, tile)
            k, v = keys(), values()
            scores = lax.dot_general(
                qs[x, here, :], k, (((1,), (1,)), ((), ())), preferred_element_type=jnp.float32
            )
            if visible is not None:
                scores = jnp.where(visible(scores.shape), scores, very_low)
            high = jnp.max(scores, axis=1, keepdims=True)
            if first:
                high = jnp.broadcast_to(high, (tile, HEAD_DIM))
            else:
                before = top[x, here, :]
                high = jnp.maximum(before, high)
            top[x, here, :] = high
            count_keys = k.shape[0]
            spread = jnp.concatenate([high] * -(-count_keys // HEAD_DIM), axis=1)[:, :count_keys]
            weights = jnp.exp2((scores - spread) * SCALE).astype(jnp.bfloat16)
            both = jnp.concatenate([v, jnp.ones_like(v)], axis=1)
            mixed = jnp.dot(weights, both, preferred_element_type=jnp.float32)
            if not first:
                factor = jnp.exp2((before - high) * SCALE)
                mixed = acc[x, here, :] * jnp.concatenate([factor, factor], axis=1) + mixed
            acc[x, here, :] = mixed

    def block(buf, slot, x):
        return lambda: buf[slot, x]

    per = parts * toks
    resp_tile, prompt_tile = resp_rows, GROUP * rows

    def resp_slot(x, slot):
        attend(
            x, block(kbuf, slot, x), block(vbuf, slot, x), 0, resp_tile, resp_rows // resp_tile,
            False, None,
        )

    def resp_middle(x):
        def both(buf):
            return lambda: buf[1:3, x].reshape(2 * chunk, HEAD_DIM)

        attend(
            x, both(kbuf), both(vbuf), 0, resp_tile, resp_rows // resp_tile, False, None,
        )

    def resp_own(x):
        def flat(buf):
            return lambda: buf[:, :, x * HEAD_DIM : (x + 1) * HEAD_DIM].reshape(per, HEAD_DIM)

        def visible(shape):
            row = lax.rem(lax.broadcasted_iota(jnp.int32, shape, 0), per)
            return lax.broadcasted_iota(jnp.int32, shape, 1) <= row

        attend(x, flat(rkb), flat(rvb), 0, resp_tile, resp_rows // resp_tile, True, visible)

    def prompt_slot(x, slot):
        def visible(shape):
            row = lax.rem(lax.broadcasted_iota(jnp.int32, shape, 0), rows) + y * rows
            return lax.broadcasted_iota(jnp.int32, shape, 1) <= row

        def run():
            attend(
                x, block(kbuf, slot, x), block(vbuf, slot, x), resp_rows, prompt_tile, 1,
                slot == 0, visible if slot == 0 else None,
            )

        if slot == 0:
            run()
        else:
            pl.when({1: zh >= 1, 2: zh == RING - 1, 3: zh >= 2}[slot])(run)

    def stack_prompt():
        for x in range(kv):
            for g in range(GROUP):
                at_col = (x * GROUP + g) * HEAD_DIM
                qs[x, pl.ds(resp_rows + g * rows, rows), :] = pq[:, at_col : at_col + HEAD_DIM]

    def stack_resp(x):
        for g in range(GROUP):
            at_col = (x * GROUP + g) * HEAD_DIM
            qs[x, pl.ds(g * per, per), :] = rqb[:, :, at_col : at_col + HEAD_DIM].reshape(
                per, HEAD_DIM
            )

    def quotient(x, begin, count):
        part = acc[x, pl.ds(begin, count), :]
        return (part[:, :HEAD_DIM] / part[:, HEAD_DIM:]).astype(jnp.bfloat16)

    def finish_resp(x):
        for g in range(GROUP):
            at_col = (x * GROUP + g) * HEAD_DIM
            rob[:, :, at_col : at_col + HEAD_DIM] = quotient(x, g * per, per).reshape(
                parts, toks, HEAD_DIM
            )

    def finish_prompt(x):
        for g in range(GROUP):
            at_col = (x * GROUP + g) * HEAD_DIM
            pob[:, at_col : at_col + HEAD_DIM] = quotient(x, resp_rows + g * rows, rows)
        part = pl.ds(x * wide, wide)
        bring(pob.at[:, part], po_ref.at[:, part])

    order = {1: "kv", -1: "vk"}

    def spread(a, x, way):
        arrived("z1", a, x, way)
        y1(a, x, 1 if way > 0 else 2)

    def pass_on(a, x, way):
        arrived("z1", a, x, way)
        send("z2", a, x)
        y1(a, x, 1 if way > 0 else 2)

    def after_z2(x):
        for a in "kv":
            arrived("z2", a, x)
            y1(a, x, 3)

    def take_resp(x):
        if x == 0:
            for d in range(parts - 1):
                arrived("rk", d)
                arrived("rv", d)
        for d in range(parts - 1):
            arrived("q", x, d)
        stack_resp(x)

    for copy in got_kv:
        copy.wait()

    def first_z(position):
        for x in range(kv):
            for way in (1, -1):
                send("z1", order[way][position], x, way)

    first_z(0)
    for x in range(kv):
        for a in "kv":
            y1(a, x, 0)
    first_z(1)
    got_pq.wait()
    stack_prompt()
    for copy in got_resp:
        copy.wait()
    pass_on("k", 0, 1)
    pass_on("v", 0, -1)
    whole(0, 0)
    pl.when(zh != 0)(lambda: prompt_slot(0, 0))
    pass_on("k", 1, 1)
    pass_on("v", 1, -1)
    swap_q(0)
    swap_kv()
    swap_q(1)
    whole(1, 0)
    pl.when(zh != 0)(lambda: prompt_slot(1, 0))
    for x in range(kv):
        spread("v", x, 1)
        spread("k", x, -1)
    after_z2(0)
    after_z2(1)
    for x in range(kv):
        take_resp(x)
        resp_own(x)
        resp_slot(x, 0)
        whole(x, 1)
        whole(x, 2)
        resp_middle(x)
    for x in range(kv):
        whole(x, 3)
        resp_slot(x, 3)
        finish_resp(x)
        swap_out(x)
    for x in range(kv):
        pl.when(zh == 0)(lambda x=x: prompt_slot(x, 0))
        for slot in range(1, RING):
            prompt_slot(x, slot)
        finish_prompt(x)
    for x in range(kv):
        for d in range(parts - 1):
            arrived("o", x, d)
    for name in number:
        message(name).wait_send()
    for copy in local[1 + len(got_kv) + len(got_resp):]:
        copy.wait()


def hand_over(toks, lengths_ref, prompt_ref, mixed_ref, prompt_out_ref, resp_out_ref, held, sems):
    copies = [
        pltpu.make_async_copy(prompt_ref, prompt_out_ref, sems.at[0]),
        pltpu.make_async_copy(mixed_ref, held, sems.at[1]),
        pltpu.make_async_copy(held, resp_out_ref, sems.at[2]),
    ]
    copies[1].start()
    copies[0].start()
    copies[1].wait()
    position = lax.axis_index("head") * toks + lax.broadcasted_iota(jnp.int32, held.shape, 0)
    mixed = held[...]
    held[...] = jnp.where(position < lengths_ref[0], mixed, jnp.zeros_like(mixed))
    copies[2].start()
    copies[0].wait()
    copies[2].wait()


def on_device(prompt_q, prompt_k, prompt_v, resp_q, resp_k, resp_v, lengths):
    rows, qwidth = prompt_q.shape
    kwidth = prompt_k.shape[1]
    toks = resp_q.shape[1]
    parts = lax.axis_size("head")
    kv = kwidth // HEAD_DIM
    total = GROUP * (rows + parts * toks)
    any_place = pl.BlockSpec(memory_space=pltpu.HBM)
    bf16 = jnp.bfloat16
    messages = 88
    plain = pl.BlockSpec(memory_space=pl.ANY)
    prompt_raw, mixed = pl.pallas_call(
        functools.partial(kernel, (rows, toks, parts)),
        out_shape=(
            pltpu.VMEM((rows, qwidth), bf16),
            pltpu.VMEM((toks, parts * qwidth), bf16),
        ),
        in_specs=[any_place] * 6,
        out_specs=(any_place, any_place),
        scratch_shapes=[
            pltpu.VMEM((RING, kv, RING * rows, HEAD_DIM), bf16),
            pltpu.VMEM((RING, kv, RING * rows, HEAD_DIM), bf16),
            pltpu.VMEM((rows, qwidth), bf16),
            pltpu.VMEM((parts, toks, qwidth), bf16),
            pltpu.VMEM((parts, toks, kwidth), bf16),
            pltpu.VMEM((parts, toks, kwidth), bf16),
            pltpu.VMEM((kv, total, HEAD_DIM), bf16),
            pltpu.VMEM((kv, total, HEAD_DIM), jnp.float32),
            pltpu.VMEM((kv, total, 2 * HEAD_DIM), jnp.float32),
            pltpu.VMEM((rows, qwidth), bf16),
            pltpu.VMEM((parts, toks, qwidth), bf16),
            pltpu.SemaphoreType.DMA((messages,)),
            pltpu.SemaphoreType.DMA((messages,)),
            pltpu.SemaphoreType.DMA((16,)),
        ],
        compiler_params=pltpu.CompilerParams(
            collective_id=0, has_side_effects=True, vmem_limit_bytes=60 * 1024 * 1024
        ),
    )(prompt_q, prompt_k, prompt_v, resp_q[0], resp_k[0], resp_v[0])
    prompt_out, resp_out = pl.pallas_call(
        functools.partial(hand_over, toks),
        out_shape=(
            jax.ShapeDtypeStruct((rows, qwidth), bf16),
            jax.ShapeDtypeStruct((toks, parts * qwidth), bf16),
        ),
        in_specs=[pl.BlockSpec(memory_space=pltpu.SMEM), plain, plain],
        out_specs=(plain, plain),
        scratch_shapes=[
            pltpu.VMEM((toks, parts * qwidth), bf16),
            pltpu.SemaphoreType.DMA((3,)),
        ],
    )(
        lengths,
        pltpu.with_memory_space_constraint(prompt_raw, pltpu.VMEM),
        pltpu.with_memory_space_constraint(mixed, pltpu.VMEM),
    )
    return (prompt_out, resp_out[None])


def solution(mesh):
    placed = (
        P(("grp", "seq"), "head"),
        P(("grp", "seq"), "head"),
        P(("grp", "seq"), "head"),
        P(("grp", "seq"), "head", None),
        P(("grp", "seq"), "head", None),
        P(("grp", "seq"), "head", None),
        P(("grp", "seq")),
    )
    return jax.shard_map(
        on_device,
        mesh=mesh,
        in_specs=placed,
        out_specs=(P(("grp", "seq"), "head"), P(("grp", "seq"), "head", None)),
        check_vma=False,
    )
```

```python
import functools
import math

import jax
import jax.numpy as jnp
from jax import lax
from jax.experimental import pallas as pl
from jax.experimental.pallas import tpu as pltpu
from jax.sharding import PartitionSpec as P

HEAD_DIM = 128
GROUP = 8
MESH = pl.DeviceIdType.MESH
SCALE = math.log2(math.e) / math.sqrt(HEAD_DIM)
very_low = -1e30

RING = 4


def kernel(
    sizes,
    pq_ref, pk_ref, pv_ref, rq_ref, rk_ref, rv_ref,
    po_ref, ro_ref,
    kbuf, vbuf, pq, rqb, rkb, rvb, qs, top, acc, pob, rob,
    send_sem, recv_sem, local_sem,
):
    rows, toks, parts = sizes
    kv = 2
    wide = GROUP * HEAD_DIM
    qwidth = kv * wide
    resp_rows = GROUP * parts * toks
    chunk = RING * rows

    seq = lax.axis_index("seq")
    head = lax.axis_index("head")
    zh, y = seq // RING, lax.rem(seq, RING)

    def at(dz, dy):
        return lax.rem(zh + dz + RING, RING) * RING + lax.rem(y + dy + RING, RING)

    z_next, z_prev = at(1, 0), at(-1, 0)
    y_next, y_prev = at(0, 1), at(0, -1)
    others = [lax.rem(head + d, parts) for d in range(1, parts)]

    along_z = {1: z_next, -1: z_prev}

    barrier = pltpu.get_barrier_semaphore()
    for peer in (z_next, z_prev, y_next, y_prev, at(0, 2)):
        pl.semaphore_signal(barrier, inc=1, device_id={"seq": peer}, device_id_type=MESH)
    for peer in others:
        pl.semaphore_signal(barrier, inc=1, device_id={"head": peer}, device_id_type=MESH)

    def rows_of(dy):
        return pl.ds(pl.multiple_of(lax.rem(y + dy + RING, RING) * rows, 16), rows)

    mine = rows_of(0)
    bufs, given = {"k": kbuf, "v": vbuf}, {"k": pk_ref, "v": pv_ref}

    local = []

    def bring(src, dst):
        copy = pltpu.make_async_copy(src, dst, local_sem.at[len(local)])
        copy.start()
        local.append(copy)
        return copy

    got_pq = bring(pq_ref, pq)
    got_kv = [
        bring(given[a].at[:, pl.ds(x * HEAD_DIM, HEAD_DIM)], bufs[a].at[0, x, mine])
        for x in range(kv)
        for a in "kv"
    ]
    own_q = pl.ds(pl.multiple_of(head * qwidth, qwidth), qwidth)
    own_kv = pl.ds(pl.multiple_of(head * kv * HEAD_DIM, kv * HEAD_DIM), kv * HEAD_DIM)
    got_resp = [
        bring(rq_ref.at[:, own_q], rqb.at[head]),
        bring(rk_ref.at[:, own_kv], rkb.at[head]),
        bring(rv_ref.at[:, own_kv], rvb.at[head]),
    ]
    pl.semaphore_wait(barrier, 5 + len(others))

    number = {}

    def message(name):
        kind, *which = name
        if kind == "z1":
            a, x, way = which
            src, dst = bufs[a].at[0, x, mine], bufs[a].at[1 if way > 0 else 2, x, mine]
            peer = {"seq": along_z[way]}
        elif kind == "z2":
            a, x = which
            slot, way = (1, 1) if a == "k" else (2, -1)
            src, dst = bufs[a].at[slot, x, mine], bufs[a].at[3, x, mine]
            peer = {"seq": along_z[way]}
        elif kind == "y":
            a, x, slot, way = which
            src = dst = bufs[a].at[slot, x, mine]
            peer = {"seq": at(0, way)}
        else:
            *x, d = which
            peer = {"head": others[d]}
            if kind == "q":
                begin = pl.multiple_of(others[d] * qwidth + x[0] * wide, wide)
                src = rq_ref.at[:, pl.ds(begin, wide)]
                dst = rqb.at[head, :, pl.ds(x[0] * wide, wide)]
            elif kind == "o":
                to = pl.multiple_of(head * qwidth + x[0] * wide, wide)
                src = rob.at[others[d], :, pl.ds(x[0] * wide, wide)]
                dst = ro_ref.at[:, pl.ds(to, wide)]
            else:
                begin = pl.multiple_of(others[d] * kv * HEAD_DIM, kv * HEAD_DIM)
                given, held = (rk_ref, rkb) if kind == "rk" else (rv_ref, rvb)
                src, dst = given.at[:, pl.ds(begin, kv * HEAD_DIM)], held.at[head]
        at_sem = number.setdefault(name, len(number))
        return pltpu.make_async_remote_copy(
            src_ref=src,
            dst_ref=dst,
            send_sem=send_sem.at[at_sem],
            recv_sem=recv_sem.at[at_sem],
            device_id=peer,
            device_id_type=MESH,
        )

    def send(*name):
        message(name).start()

    def arrived(*name):
        message(name).wait_recv()

    def y1(a, x, slot):
        for way in (1, -1, 2) if a == "k" else (-1, 1, 2):
            send("y", a, x, slot, way)

    def whole(x, slot):
        for way in (1, -1, 2):
            for a in "kv":
                arrived("y", a, x, slot, way)

    def swap_q(x):
        for d in range(parts - 1):
            send("q", x, d)

    def swap_kv():
        for d in range(parts - 1):
            send("rk", d)
            send("rv", d)

    def swap_out(x):
        for d in range(parts - 1):
            send("o", x, d)
        to = pl.multiple_of(head * qwidth + x * wide, wide)
        bring(rob.at[head, :, pl.ds(x * wide, wide)], ro_ref.at[:, pl.ds(to, wide)])

    def attend(x, keys, values, begin, tile, count, first, visible):
        for i in range(count):
            here = pl.ds(begin + i * tile, tile)
            k, v = keys(), values()
            scores = lax.dot_general(
                qs[x, here, :], k, (((1,), (1,)), ((), ())), preferred_element_type=jnp.float32
            )
            if visible is not None:
                scores = jnp.where(visible(scores.shape), scores, very_low)
            high = jnp.max(scores, axis=1, keepdims=True)
            if first:
                high = jnp.broadcast_to(high, (tile, HEAD_DIM))
            else:
                before = top[x, here, :]
                high = jnp.maximum(before, high)
            top[x, here, :] = high
            count_keys = k.shape[0]
            spread = jnp.concatenate([high] * -(-count_keys // HEAD_DIM), axis=1)[:, :count_keys]
            weights = jnp.exp2((scores - spread) * SCALE).astype(jnp.bfloat16)
            both = jnp.concatenate([v, jnp.ones_like(v)], axis=1)
            mixed = jnp.dot(weights, both, preferred_element_type=jnp.float32)
            if not first:
                factor = jnp.exp2((before - high) * SCALE)
                mixed = acc[x, here, :] * jnp.concatenate([factor, factor], axis=1) + mixed
            acc[x, here, :] = mixed

    def block(buf, slot, x):
        return lambda: buf[slot, x]

    per = parts * toks
    resp_tile, prompt_tile = resp_rows, GROUP * rows

    def resp_slot(x, slot):
        attend(
            x, block(kbuf, slot, x), block(vbuf, slot, x), 0, resp_tile, resp_rows // resp_tile,
            False, None,
        )

    def resp_middle(x):
        def both(buf):
            return lambda: buf[1:3, x].reshape(2 * chunk, HEAD_DIM)

        attend(
            x, both(kbuf), both(vbuf), 0, resp_tile, resp_rows // resp_tile, False, None,
        )

    def resp_first(x):
        def joined(buf, own):
            return lambda: jnp.concatenate(
                [buf[0, x], own[:, :, x * HEAD_DIM : (x + 1) * HEAD_DIM].reshape(per, HEAD_DIM)],
                axis=0,
            )

        def visible(shape):
            row = lax.rem(lax.broadcasted_iota(jnp.int32, shape, 0), per)
            return lax.broadcasted_iota(jnp.int32, shape, 1) - chunk <= row

        attend(
            x, joined(kbuf, rkb), joined(vbuf, rvb), 0, resp_tile, resp_rows // resp_tile, True,
            visible,
        )

    def prompt_slot(x, slot):
        def visible(shape):
            row = lax.rem(lax.broadcasted_iota(jnp.int32, shape, 0), rows) + y * rows
            return lax.broadcasted_iota(jnp.int32, shape, 1) <= row

        def run():
            attend(
                x, block(kbuf, slot, x), block(vbuf, slot, x), resp_rows, prompt_tile, 1,
                slot == 0, visible if slot == 0 else None,
            )

        if slot == 0:
            run()
        else:
            pl.when({1: zh >= 1, 2: zh == RING - 1, 3: zh >= 2}[slot])(run)

    def stack_prompt():
        for x in range(kv):
            for g in range(GROUP):
                at_col = (x * GROUP + g) * HEAD_DIM
                qs[x, pl.ds(resp_rows + g * rows, rows), :] = pq[:, at_col : at_col + HEAD_DIM]

    def stack_resp(x):
        for g in range(GROUP):
            at_col = (x * GROUP + g) * HEAD_DIM
            qs[x, pl.ds(g * per, per), :] = rqb[:, :, at_col : at_col + HEAD_DIM].reshape(
                per, HEAD_DIM
            )

    def quotient(x, begin, count):
        part = acc[x, pl.ds(begin, count), :]
        return (part[:, :HEAD_DIM] / part[:, HEAD_DIM:]).astype(jnp.bfloat16)

    def finish_resp(x):
        for g in range(GROUP):
            at_col = (x * GROUP + g) * HEAD_DIM
            rob[:, :, at_col : at_col + HEAD_DIM] = quotient(x, g * per, per).reshape(
                parts, toks, HEAD_DIM
            )

    def finish_prompt(x):
        for g in range(GROUP):
            at_col = (x * GROUP + g) * HEAD_DIM
            pob[:, at_col : at_col + HEAD_DIM] = quotient(x, resp_rows + g * rows, rows)
        part = pl.ds(x * wide, wide)
        bring(pob.at[:, part], po_ref.at[:, part])

    order = {1: "kv", -1: "vk"}

    def spread(a, x, way):
        arrived("z1", a, x, way)
        y1(a, x, 1 if way > 0 else 2)

    def pass_on(a, x, way):
        arrived("z1", a, x, way)
        send("z2", a, x)
        y1(a, x, 1 if way > 0 else 2)

    def after_z2(x):
        for a in "kv":
            arrived("z2", a, x)
            y1(a, x, 3)

    def take_resp(x):
        if x == 0:
            for d in range(parts - 1):
                arrived("rk", d)
                arrived("rv", d)
        for d in range(parts - 1):
            arrived("q", x, d)
        stack_resp(x)

    for copy in got_kv:
        copy.wait()

    def first_z(position):
        for x in range(kv):
            for way in (1, -1):
                send("z1", order[way][position], x, way)

    first_z(0)
    for x in range(kv):
        for a in "kv":
            y1(a, x, 0)
    first_z(1)
    got_pq.wait()
    stack_prompt()
    for copy in got_resp:
        copy.wait()
    pass_on("k", 0, 1)
    pass_on("v", 0, -1)
    whole(0, 0)
    pl.when(zh != 0)(lambda: prompt_slot(0, 0))
    pass_on("k", 1, 1)
    pass_on("v", 1, -1)
    swap_q(0)
    swap_kv()
    swap_q(1)
    whole(1, 0)
    pl.when(zh != 0)(lambda: prompt_slot(1, 0))
    for x in range(kv):
        spread("v", x, 1)
        spread("k", x, -1)
    after_z2(0)
    after_z2(1)
    for x in range(kv):
        take_resp(x)
        resp_first(x)
        whole(x, 1)
        whole(x, 2)
        resp_middle(x)
    for x in range(kv):
        whole(x, 3)
        resp_slot(x, 3)
        finish_resp(x)
        swap_out(x)
    for x in range(kv):
        pl.when(zh == 0)(lambda x=x: prompt_slot(x, 0))
        for slot in range(1, RING):
            prompt_slot(x, slot)
        finish_prompt(x)
    for x in range(kv):
        for d in range(parts - 1):
            arrived("o", x, d)
    for name in number:
        message(name).wait_send()
    for copy in local[1 + len(got_kv) + len(got_resp):]:
        copy.wait()


def hand_over(toks, lengths_ref, prompt_ref, mixed_ref, prompt_out_ref, resp_out_ref, held, sems):
    copies = [
        pltpu.make_async_copy(prompt_ref, prompt_out_ref, sems.at[0]),
        pltpu.make_async_copy(mixed_ref, held, sems.at[1]),
        pltpu.make_async_copy(held, resp_out_ref, sems.at[2]),
    ]
    copies[1].start()
    copies[0].start()
    copies[1].wait()
    position = lax.axis_index("head") * toks + lax.broadcasted_iota(jnp.int32, held.shape, 0)
    mixed = held[...]
    held[...] = jnp.where(position < lengths_ref[0], mixed, jnp.zeros_like(mixed))
    copies[2].start()
    copies[0].wait()
    copies[2].wait()


def on_device(prompt_q, prompt_k, prompt_v, resp_q, resp_k, resp_v, lengths):
    rows, qwidth = prompt_q.shape
    kwidth = prompt_k.shape[1]
    toks = resp_q.shape[1]
    parts = lax.axis_size("head")
    kv = kwidth // HEAD_DIM
    total = GROUP * (rows + parts * toks)
    any_place = pl.BlockSpec(memory_space=pltpu.HBM)
    bf16 = jnp.bfloat16
    messages = 88
    plain = pl.BlockSpec(memory_space=pl.ANY)
    prompt_raw, mixed = pl.pallas_call(
        functools.partial(kernel, (rows, toks, parts)),
        out_shape=(
            pltpu.VMEM((rows, qwidth), bf16),
            pltpu.VMEM((toks, parts * qwidth), bf16),
        ),
        in_specs=[any_place] * 6,
        out_specs=(any_place, any_place),
        scratch_shapes=[
            pltpu.VMEM((RING, kv, RING * rows, HEAD_DIM), bf16),
            pltpu.VMEM((RING, kv, RING * rows, HEAD_DIM), bf16),
            pltpu.VMEM((rows, qwidth), bf16),
            pltpu.VMEM((parts, toks, qwidth), bf16),
            pltpu.VMEM((parts, toks, kwidth), bf16),
            pltpu.VMEM((parts, toks, kwidth), bf16),
            pltpu.VMEM((kv, total, HEAD_DIM), bf16),
            pltpu.VMEM((kv, total, HEAD_DIM), jnp.float32),
            pltpu.VMEM((kv, total, 2 * HEAD_DIM), jnp.float32),
            pltpu.VMEM((rows, qwidth), bf16),
            pltpu.VMEM((parts, toks, qwidth), bf16),
            pltpu.SemaphoreType.DMA((messages,)),
            pltpu.SemaphoreType.DMA((messages,)),
            pltpu.SemaphoreType.DMA((16,)),
        ],
        compiler_params=pltpu.CompilerParams(
            collective_id=0, has_side_effects=True, vmem_limit_bytes=60 * 1024 * 1024
        ),
    )(prompt_q, prompt_k, prompt_v, resp_q[0], resp_k[0], resp_v[0])
    prompt_out, resp_out = pl.pallas_call(
        functools.partial(hand_over, toks),
        out_shape=(
            jax.ShapeDtypeStruct((rows, qwidth), bf16),
            jax.ShapeDtypeStruct((toks, parts * qwidth), bf16),
        ),
        in_specs=[pl.BlockSpec(memory_space=pltpu.SMEM), plain, plain],
        out_specs=(plain, plain),
        scratch_shapes=[
            pltpu.VMEM((toks, parts * qwidth), bf16),
            pltpu.SemaphoreType.DMA((3,)),
        ],
    )(
        lengths,
        pltpu.with_memory_space_constraint(prompt_raw, pltpu.VMEM),
        pltpu.with_memory_space_constraint(mixed, pltpu.VMEM),
    )
    return (prompt_out, resp_out[None])


def solution(mesh):
    placed = (
        P(("grp", "seq"), "head"),
        P(("grp", "seq"), "head"),
        P(("grp", "seq"), "head"),
        P(("grp", "seq"), "head", None),
        P(("grp", "seq"), "head", None),
        P(("grp", "seq"), "head", None),
        P(("grp", "seq")),
    )
    return jax.shard_map(
        on_device,
        mesh=mesh,
        in_specs=placed,
        out_specs=(P(("grp", "seq"), "head"), P(("grp", "seq"), "head", None)),
        check_vma=False,
    )
```
